256 devices in a mesh: hour: 32 (over z_hi, x, y), site: 8 (over z_lo, core).
Axes of the slice: x: 4, y: 4, z: 8 (z_hi: 2, z_lo: 4; z = z_hi * 4 + z_lo), core: 2. Of those that a mesh axis runs over, the one named last changes fastest.
Arguments:
- fields: bfloat16 [5120, 20480], P('hour', 'site'), may hold values from -6 to 6
- time_basis: bfloat16 [5120, 1536], P('hour'), may hold values from -0.15625 to 0.15625
- features: bfloat16 [20480, 2048], P('site'), may hold values from -0.1875 to 0.1875
- time_spectrum: float32 [1536], replicated, may hold values from 0.05 to 5
- feature_spectrum: float32 [2048], replicated, may hold values from 0.05 to 5
Outputs:
- solved: bfloat16 [5120, 20480], P('hour', 'site')
The draws below stay inside these ranges and needn't reach their ends.
All inputs are finite; a program needn't handle non-finite values.
Results may differ from the reference program's by a relative error of at most 0.009.
Values may be sent and summed in bfloat16 or wider, within the bound.
A program may use at most 64 MiB of HBM per device.

```python
import math
import jax
import jax.numpy as jnp

FEAT = 2048
HOURS = 5120
SITES = 20480
BASIS = 1536


def with_spikes(drawn, own_key, source, target, blocks, factor):
    def block_of(dim):
        return (jnp.arange(drawn.shape[dim]) // (drawn.shape[dim] // blocks)).reshape((-1,) + (1,) * (drawn.ndim - 1 - dim))

    one_side = jax.random.permutation(own_key, blocks)[block_of(target)]
    second = (block_of(target) + blocks // 2) % blocks
    return jnp.where((block_of(source) == one_side) | (block_of(source) == second), factor * drawn, drawn)


def block_levels(stream_key, extent, split, smallest, top_value):
    def one(axis_at, shards_of):
        draws = jax.random.uniform(jax.random.fold_in(jax.random.fold_in(stream_key, 6), axis_at), (shards_of,), jnp.float32, smallest / len(split), top_value / len(split))
        return jnp.repeat(jnp.exp(draws), extent[axis_at] // shards_of).reshape((-1,) + (1,) * (len(extent) - axis_at - 1))

    level = one(*split[0])
    for cut in split[1:]:
        level = level * one(*cut)
    return level


def scatter_about(own_key, dims, scale, bound, split=(), held_as=jnp.bfloat16):
    entries = scale * jax.random.normal(own_key, dims, jnp.float32)
    if split:
        entries = entries * block_levels(own_key, dims, split, -0.22, 0.18)
    return jnp.clip(entries, -bound, bound).astype(held_as)


def heavy_noise(stream_key, extent, deviation, limit, shards, heavy, dtype=jnp.bfloat16):
    array = deviation * jax.random.normal(stream_key, extent, jnp.float32)
    if shards:
        array = array * block_levels(stream_key, extent, shards, -0.22, 0.18)
    return jnp.clip(with_spikes(array, jax.random.fold_in(stream_key, 3), *heavy), -limit, limit).astype(dtype)


def setup_inputs(seed: int = 0) -> dict:
    seeds = jax.random.split(jax.random.key(seed), 6)
    return {
        "fields": scatter_about(seeds[0], (HOURS, SITES), 1.0, 6.0, ((0, 32), (1, 8))),
        "time_basis": heavy_noise(seeds[1], (HOURS, BASIS), HOURS ** -0.5, 0.15625, ((0, 32),), (0, 1, 32, 2.75)),
        "features": heavy_noise(seeds[2], (SITES, FEAT), FEAT ** -0.5, 0.1875, ((0, 8),), (0, 1, 8, 2.0)),
        "time_spectrum": jnp.clip(jnp.exp(jax.random.uniform(seeds[3], (BASIS,), jnp.float32, math.log(0.05), math.log(5.0))), 0.05, 5.0),
        "feature_spectrum": jnp.clip(jnp.exp(jax.random.uniform(seeds[4], (FEAT,), jnp.float32, math.log(0.05), math.log(5.0))), 0.05, 5.0),
    }


noise_var = 0.1


def reference(fields, time_basis, features, time_spectrum, feature_spectrum):
    projected = jnp.dot(fields, features, preferred_element_type=jnp.float32).astype(jnp.bfloat16)
    coefficients = jnp.dot(time_basis.T, projected, preferred_element_type=jnp.float32)
    denominator = time_spectrum[:, None] + feature_spectrum[None, :] + noise_var
    scaled = (coefficients / denominator).astype(jnp.bfloat16)
    mixed = jnp.dot(time_basis, scaled, preferred_element_type=jnp.float32).astype(jnp.bfloat16)
    return jnp.dot(mixed, features.T, preferred_element_type=jnp.float32).astype(jnp.bfloat16)
```

```python
import jax
import jax.numpy as jnp
from jax import lax
from jax.experimental import pallas as pl
from jax.experimental.pallas import tpu as pltpu
from jax.sharding import PartitionSpec as P

noise_var = 0.1

RING = 8
PLANE = 16
FAR_FIRST = (4, 3, 5, 2, 6, 1, 7, 0)
NEAR_FIRST = (0, 1, 7, 2, 6, 3, 5, 4)
PLANE_FAR_FIRST = (10, 6, 14, 9, 11, 2, 8, 5, 7, 13, 15, 1, 3, 4, 12)
f32 = jnp.float32
bf16 = jnp.bfloat16


def kernel(fields, basis, features, ts_ref, fs_ref, out,
           feats, fbuf, t2, tt, cx_own, cx_send, cx_recv, zs_send, zs_recv,
           c_send, c_recv, s_own, s_all, m_send, m_all, acc, tcol,
           load_sem, feat_sem, t_send_sem, t_recv_sem, cx_ssem, cx_rsem, zs_ssem, zs_rsem,
           c_ssem, c_rsem, s_ssem, s_rsem, m_ssem, m_rsem, f_ssem, f_rsem):
    hour, site = lax.axis_index("hour"), lax.axis_index("site")
    zh, x, y = hour // 16, (hour // 4) % 4, hour % 4
    zl, core = site // 2, site % 2
    z = zh * 4 + zl
    rows = fields.shape[0]
    part = c_send.shape[0] // PLANE

    def at(z_, x_, y_, c_):
        return (((z_ // 4) * 4 + x_) * 4 + y_, (z_ % 4) * 2 + c_)

    def ring(d):
        return at((z + d) % RING, x, y, core)

    def plane(q):
        return at(z, (x + q // 4) % 4, (y + q % 4) % 4, core)

    sibling = at(z, x, y, 1 - core)

    def send(src, dst, ssem, rsem, device):
        copy = pltpu.make_async_remote_copy(
            src_ref=src, dst_ref=dst, send_sem=ssem, recv_sem=rsem,
            device_id=device, device_id_type=pl.DeviceIdType.MESH)
        copy.start()
        return copy

    barrier = pltpu.get_barrier_semaphore()
    for d in range(1, RING):
        pl.semaphore_signal(barrier, inc=1, device_id=ring(d), device_id_type=pl.DeviceIdType.MESH)
    for q in range(1, PLANE):
        pl.semaphore_signal(barrier, inc=1, device_id=plane(q), device_id_type=pl.DeviceIdType.MESH)
    pl.semaphore_signal(barrier, inc=1, device_id=sibling, device_id_type=pl.DeviceIdType.MESH)

    load_f = pltpu.make_async_copy(fields, fbuf, load_sem.at[0])
    load_f.start()
    own_t = pl.ds(pl.multiple_of(zh * rows, rows), rows)
    load_t = pltpu.make_async_copy(basis, t2.at[own_t], load_sem.at[1])
    loads = {}
    for i, d in enumerate(FAR_FIRST):
        col = pl.multiple_of(((z + d) % RING) * 256, 256)
        loads[d] = pltpu.make_async_copy(features.at[:, pl.ds(col, 256)], feats.at[d], feat_sem.at[d])
        loads[d].start()
        if i == 0:
            load_t.start()

    tcol[...] = jnp.broadcast_to(ts_ref[...], (128, ts_ref.shape[1])).T

    load_f.wait()
    load_t.wait()
    pl.semaphore_wait(barrier, RING - 1 + PLANE - 1 + 1)

    half = rows // 2
    mine_t = pl.ds(pl.multiple_of(zh * rows + core * half, half), half)
    near = (zl == 0) | (zl == 3)
    edge = jnp.where(zl == 0, -1, 1)
    edge_dev = at((z + edge + RING) % RING, x, y, core)
    inner_dev = at((z - edge + RING) % RING, x, y, core)
    other_t = pl.ds(pl.multiple_of((1 - zh) * rows + core * half, half), half)
    other_t2 = pl.ds(pl.multiple_of((1 - zh) * rows + (1 - core) * half, half), half)

    t_out = pltpu.make_async_remote_copy(
        src_ref=t2.at[mine_t], dst_ref=t2.at[mine_t], send_sem=t_send_sem.at[0], recv_sem=t_recv_sem.at[0],
        device_id=edge_dev, device_id_type=pl.DeviceIdType.MESH)
    t_in = pltpu.make_async_remote_copy(
        src_ref=t2.at[other_t], dst_ref=t2.at[other_t], send_sem=t_send_sem.at[1], recv_sem=t_recv_sem.at[0],
        device_id=inner_dev, device_id_type=pl.DeviceIdType.MESH)
    t_sib = pltpu.make_async_remote_copy(
        src_ref=t2.at[other_t], dst_ref=t2.at[other_t], send_sem=t_send_sem.at[2], recv_sem=t_recv_sem.at[1],
        device_id=sibling, device_id_type=pl.DeviceIdType.MESH)

    @pl.when(near)
    def _():
        t_out.start()

    cx, zs = {}, {}

    def mm1(d):
        loads[d].wait()
        block = jnp.dot(fbuf[...], feats[d], preferred_element_type=f32)
        low, high = block[:, :128], block[:, 128:]
        first = core == 0
        cx_own[d] = jnp.where(first, low, high)
        cx_send[d] = jnp.where(first, high, low).astype(bf16)
        cx[d] = send(cx_send.at[d], cx_recv.at[d], cx_ssem.at[d], cx_rsem.at[d], sibling)

    def pass_on(d):
        cx[d].wait_recv()
        total = (cx_own[d] + cx_recv[d].astype(f32)).astype(bf16)
        if d == 0:
            zs_recv[z] = total
        else:
            zs_send[d] = total
            zs[d] = send(zs_send.at[d], zs_recv.at[z], zs_ssem.at[d], zs_rsem.at[d], ring(d))

    SKEW = 2
    for i in range(RING + SKEW):
        if i < RING:
            mm1(FAR_FIRST[i])
        if i >= SKEW:
            pass_on(FAR_FIRST[i - SKEW])

    t_out.wait_recv()

    @pl.when(near)
    def _():
        t_in.start()

    t_sib.start()
    t_sib.wait_recv()
    tt[...] = t2[...].T

    for d in range(1, RING):
        zs[d].wait_recv()
    sum_a = (zs_recv[0].astype(f32) + zs_recv[1].astype(f32)) + (zs_recv[2].astype(f32) + zs_recv[3].astype(f32))
    sum_b = (zs_recv[4].astype(f32) + zs_recv[5].astype(f32)) + (zs_recv[6].astype(f32) + zs_recv[7].astype(f32))
    projected = jnp.concatenate([sum_a.astype(bf16), sum_b.astype(bf16)], axis=0)

    c_send[...] = jnp.dot(tt[...], projected, preferred_element_type=f32).astype(bf16)
    cs = {}
    for q in PLANE_FAR_FIRST:
        target = ((x + q // 4) % 4) * 4 + (y + q % 4) % 4
        src = c_send.at[pl.ds(pl.multiple_of(target * part, part), part)]
        cs[q] = send(src, c_recv.at[q], c_ssem.at[q], c_rsem.at[q], plane(q))
    own_r = pl.ds(pl.multiple_of((x * 4 + y) * part, part), part)
    total = c_send[own_r].astype(f32)
    col = pl.multiple_of(z * 256 + core * 128, 128)
    denom = tcol[own_r] + fs_ref[:, pl.ds(col, 128)] + noise_var
    for q in reversed(PLANE_FAR_FIRST):
        cs[q].wait_recv()
        total = total + c_recv[q].astype(f32)
    scaled = (total / denom).astype(bf16)
    s_own[...] = scaled
    s_all[own_r] = scaled
    ss = {}
    for q in PLANE_FAR_FIRST:
        ss[q] = send(s_own, s_all.at[own_r], s_ssem.at[q], s_rsem.at[q], plane(q))
    for q in reversed(PLANE_FAR_FIRST):
        ss[q].wait_recv()

    m_send[...] = jnp.dot(t2[...], s_all[...], preferred_element_type=f32).astype(bf16)
    ms = {}
    for d in FAR_FIRST[:-1]:
        dest = (z + d) % RING
        src = m_send.at[pl.ds(pl.multiple_of((dest // 4) * rows, rows), rows)]
        ms[d] = send(src, m_all.at[(RING - d) % RING, core], m_ssem.at[d], m_rsem.at[d], ring(d))
    m_all[0, core] = m_send[own_t]
    fw = {}

    def forward(d):
        if d:
            ms[RING - d].wait_recv()
        fw[d] = send(m_all.at[d, core], m_all.at[d, core], f_ssem.at[d], f_rsem.at[d], sibling)

    def mm4(d):
        fw[d].wait_recv()
        block = jnp.concatenate([m_all[d, 0], m_all[d, 1]], axis=1)
        add = lax.dot_general(block, feats[d], (((1,), (1,)), ((), ())), preferred_element_type=f32)
        if d == NEAR_FIRST[0]:
            acc[...] = add
        elif d == NEAR_FIRST[-1]:
            out[...] = (acc[...] + add).astype(out.dtype)
        else:
            acc[...] += add

    for i in range(RING + 1):
        if i < RING:
            forward(NEAR_FIRST[i])
        if i >= 1:
            mm4(NEAR_FIRST[i - 1])

    @pl.when(near)
    def _():
        t_out.wait_send()
        t_in.wait_send()

    t_sib.wait_send()
    for copies in (cx, zs, cs, ss, ms, fw):
        for copy in copies.values():
            copy.wait_send()


def per_device(fields, basis, features, time_spectrum, feature_spectrum):
    rows, sites = fields.shape
    n_basis = basis.shape[1]
    part = n_basis // PLANE
    any_space = pl.BlockSpec(memory_space=pl.ANY)
    vmem = pl.BlockSpec(memory_space=pltpu.VMEM)
    dma = pltpu.SemaphoreType.DMA
    return pl.pallas_call(
        kernel,
        out_shape=jax.ShapeDtypeStruct((rows, sites), bf16),
        in_specs=[any_space, any_space, any_space, vmem, vmem],
        out_specs=vmem,
        scratch_shapes=[
            pltpu.VMEM((RING, sites, 256), bf16),
            pltpu.VMEM((rows, sites), bf16),
            pltpu.VMEM((2 * rows, n_basis), bf16),
            pltpu.VMEM((n_basis, 2 * rows), bf16),
            pltpu.VMEM((RING, rows, 128), f32),
            pltpu.VMEM((RING, rows, 128), bf16),
            pltpu.VMEM((RING, rows, 128), bf16),
            pltpu.VMEM((RING, rows, 128), bf16),
            pltpu.VMEM((RING, rows, 128), bf16),
            pltpu.VMEM((n_basis, 128), bf16),
            pltpu.VMEM((PLANE, part, 128), bf16),
            pltpu.VMEM((part, 128), bf16),
            pltpu.VMEM((n_basis, 128), bf16),
            pltpu.VMEM((2 * rows, 128), bf16),
            pltpu.VMEM((RING, 2, rows, 128), bf16),
            pltpu.VMEM((rows, sites), f32),
            pltpu.VMEM((n_basis, 128), f32),
            dma((2,)), dma((RING,)), dma((3,)), dma((2,)),
            dma((RING,)), dma((RING,)), dma((RING,)), dma((RING,)),
            dma((PLANE,)), dma((PLANE,)), dma((PLANE,)), dma((PLANE,)),
            dma((RING,)), dma((RING,)), dma((RING,)), dma((RING,)),
        ],
        compiler_params=pltpu.CompilerParams(
            collective_id=0, has_side_effects=True, vmem_limit_bytes=48 * 2**20),
        cost_estimate=pl.CostEstimate(flops=3_600_000_000, bytes_accessed=13_000_000, transcendentals=0),
        name="solve",
    )(fields, basis, features, time_spectrum.reshape(1, -1), feature_spectrum.reshape(1, -1))


def solution(mesh):
    in_specs = (P("hour", "site"), P("hour", None), P("site", None), P(), P())
    out_specs = P("hour", "site")
    return jax.shard_map(
        per_device, mesh=mesh, in_specs=in_specs, out_specs=out_specs, check_vma=False
    )
```

```python
import jax
import jax.numpy as jnp
from jax import lax
from jax.experimental import pallas as pl
from jax.experimental.pallas import tpu as pltpu
from jax.sharding import PartitionSpec as P

noise_var = 0.1

RING = 8
PAIRS = 4
PLANE = 16
CHUNKS = 2
LANES = 128
PAIR_ORDER = (2, 1, 3, 0)
PLANE_FAR_FIRST = (10, 6, 14, 9, 11, 2, 8, 5, 7, 13, 15, 1, 3, 4, 12)
f32 = jnp.float32
bf16 = jnp.bfloat16


def kernel(fields, basis, features, ts_hbm, fs_hbm, out,
           ts_ref, fs_ref, feats, featst, fbuf, t2, tt, tcol, acc,
           cx_own, cx_send, cx_recv, zs_send, zs_recv,
           c_send, c_recv, s_own, s_all, m_send, m_all,
           load_sem, feat_sem, t_ssem, t_rsem, u_ssem, u_rsem, cx_ssem, cx_rsem,
           zs_ssem, zs_rsem, c_ssem, c_rsem, s_ssem, s_rsem, m_ssem, m_rsem, f_ssem, f_rsem):
    hour, site = lax.axis_index("hour"), lax.axis_index("site")
    zh, x, y = hour // 16, (hour // 4) % 4, hour % 4
    zl, core = site // 2, site % 2
    z = zh * 4 + zl
    odd = z % 2
    rows = fields.shape[0]
    half = rows // 2
    n_basis = basis.shape[1]
    mid = n_basis // 2
    width = features.shape[1] // CHUNKS
    part = mid // PLANE
    left = lax.broadcasted_iota(jnp.int32, (1, LANES), 1) < LANES // 2

    def at(z_, x_, y_, c_):
        return (((z_ // 4) * 4 + x_) * 4 + y_, (z_ % 4) * 2 + c_)

    def ring(z_):
        return at(z_, x, y, core)

    def plane(q):
        return at(z, (x + q // 4) % 4, (y + q % 4) % 4, core)

    def in_pair(m, e):
        return ((z // 2 + m) % PAIRS) * 2 + e

    sibling = at(z, x, y, 1 - core)

    def remote(src, dst, ssem, rsem, device):
        return pltpu.make_async_remote_copy(
            src_ref=src, dst_ref=dst, send_sem=ssem, recv_sem=rsem,
            device_id=device, device_id_type=pl.DeviceIdType.MESH)

    def send(*args):
        copy = remote(*args)
        copy.start()
        return copy

    def swap(v):
        return pltpu.roll(v, LANES // 2, axis=1)

    barrier = pltpu.get_barrier_semaphore()
    for d in range(1, RING):
        pl.semaphore_signal(barrier, inc=1, device_id=ring((z + d) % RING), device_id_type=pl.DeviceIdType.MESH)
    for q in range(1, PLANE):
        pl.semaphore_signal(barrier, inc=1, device_id=plane(q), device_id_type=pl.DeviceIdType.MESH)
    pl.semaphore_signal(barrier, inc=1, device_id=sibling, device_id_type=pl.DeviceIdType.MESH)

    load_t = pltpu.make_async_copy(basis, t2.at[0], load_sem.at[1])
    load_t.start()
    load_f = pltpu.make_async_copy(fields, fbuf, load_sem.at[0])
    load_f.start()
    load_ts = pltpu.make_async_copy(ts_hbm, ts_ref, load_sem.at[2])
    load_ts.start()
    load_fs = pltpu.make_async_copy(fs_hbm, fs_ref, load_sem.at[3])
    load_fs.start()
    loads = {}
    for k in range(CHUNKS):
        for m in PAIR_ORDER:
            col = pl.multiple_of(k * width + ((z // 2 + m) % PAIRS) * 256, 256)
            loads[k, m] = pltpu.make_async_copy(
                features.at[:, pl.ds(col, 256)], feats.at[k, m], feat_sem.at[k, m])
            loads[k, m].start()

    load_ts.wait()
    load_fs.wait()
    tcol[...] = jnp.broadcast_to(ts_ref[...][None, :], (LANES, n_basis)).T
    load_t.wait()
    pl.semaphore_wait(barrier, RING - 1 + PLANE - 1 + 1)

    near = (zl == 0) | (zl == 3)
    edge = jnp.where(zl == 0, RING - 1, 1)
    edge_dev = ring((z + edge) % RING)
    inner_dev = ring((z + RING - edge) % RING)
    my_half = pl.ds(pl.multiple_of(core * half, half), half)
    t_out, t_on, t_sib = [], [], []
    for i in range(2):
        piece = pl.ds(i * mid, mid)
        mine, other = t2.at[0, my_half, piece], t2.at[1, my_half, piece]
        t_out.append(remote(mine, other, t_ssem.at[0, i], t_rsem.at[i], edge_dev))
        t_on.append(remote(other, other, t_ssem.at[1, i], t_rsem.at[i], inner_dev))
        t_sib.append(remote(other, other, u_ssem.at[i], u_rsem.at[i], sibling))

    @pl.when(near)
    def _():
        t_out[0].start()
        t_out[1].start()

    load_f.wait()
    cx, zs = {}, {}

    def mm1(k, m):
        loads[k, m].wait()
        block = jnp.dot(fbuf[...], feats[k, m], preferred_element_type=f32)
        for e in range(2):
            top, low = block[:half, e * LANES:(e + 1) * LANES], block[half:, e * LANES:(e + 1) * LANES]
            first = jnp.where(left, top, swap(low))
            second = jnp.where(left, swap(top), low)
            cx_own[k, m, e] = jnp.where(core == 0, first, second)
            cx_send[k, m, e] = jnp.where(core == 0, second, first)
        cx[k, m] = send(cx_send.at[k, m], cx_recv.at[k, m], cx_ssem.at[k, m], cx_rsem.at[k, m], sibling)

    def pass_on(k, m):
        cx[k, m].wait_recv()
        if m:
            for e in range(2):
                zs_send[k, m, e] = (cx_own[k, m, e] + cx_recv[k, m, e]).astype(bf16)
                zs[k, m, e] = send(zs_send.at[k, m, e], zs_recv.at[k, z], zs_ssem.at[k, m, e],
                                   zs_rsem.at[k, PAIRS - m, odd], ring(in_pair(m, e)))
        else:
            zs_send[k, 0, 0] = (cx_own[k, 0, 1 - odd] + cx_recv[k, 0, 1 - odd]).astype(bf16)
            zs[k, 0, 0] = send(zs_send.at[k, 0, 0], zs_recv.at[k, z], zs_ssem.at[k, 0, 0],
                               zs_rsem.at[k, 0, odd], ring(in_pair(0, 1 - odd)))
            zs_recv[k, z] = (cx_own[k, 0, odd] + cx_recv[k, 0, odd]).astype(bf16)

    SKEW = 3
    blocks = [(k, m) for k in range(CHUNKS) for m in PAIR_ORDER]
    for i in range(len(blocks)):
        mm1(*blocks[i])
        if SKEW <= i < SKEW + PAIRS:
            pass_on(*blocks[i - SKEW])

    def t_arrived(i):
        t_out[i].wait_recv()
        t_sib[i].start()

    @pl.when(near)
    def _():
        for i in range(2):
            t_out[i].wait_recv()
            t_on[i].start()
            t_sib[i].start()

    tt[0] = t2[0].T
    for k in range(1, CHUNKS):
        for copy in [c for (kk, *_), c in zs.items() if kk == k - 1]:
            copy.wait_send()
        for m in PAIR_ORDER:
            pass_on(k, m)

    @pl.when(jnp.logical_not(near))
    def _():
        for i in range(2):
            t_out[i].wait_recv()
            t_sib[i].start()

    for i in range(2):
        t_sib[i].wait_recv()
    tt[1] = t2[1].T

    cs, ss, ms, fw = {}, {}, {}, {}

    def wait_ring(k, sem, src, dst):
        for m in range(PAIRS):
            for e in range(2):
                if m:
                    remote(src, dst, sem.at[k, m, e], sem.at[k, m, e], sibling).wait_recv()
        other = sem.at[k, 0, 1 - odd]
        remote(src, dst, other, other, sibling).wait_recv()

    def mm2(k):
        wait_ring(k, zs_rsem, zs_send.at[k, 0, 0], zs_recv.at[k, 0])
        total = None
        for g in range(2):
            base = (zh if g == 0 else 1 - zh) * 4
            packed = ((zs_recv[k, base].astype(f32) + zs_recv[k, base + 1].astype(f32))
                      + (zs_recv[k, base + 2].astype(f32) + zs_recv[k, base + 3].astype(f32)))
            swapped = swap(packed)
            low = jnp.concatenate([jnp.where(left, packed, 0), jnp.where(left, swapped, 0)], axis=0).astype(bf16)
            high = jnp.concatenate([jnp.where(left, 0, swapped), jnp.where(left, 0, packed)], axis=0).astype(bf16)
            add = (jnp.dot(tt[g, :mid], low, preferred_element_type=f32)
                   + jnp.dot(tt[g, mid:], high, preferred_element_type=f32))
            total = add if total is None else total + add
        c_send[k] = total.astype(bf16)
        for q in PLANE_FAR_FIRST:
            target = ((x + q // 4) % 4) * 4 + (y + q % 4) % 4
            src = c_send.at[k, pl.ds(pl.multiple_of(target * part, part), part)]
            cs[k, q] = send(src, c_recv.at[k, q], c_ssem.at[k, q], c_rsem.at[k, q], plane(q))

    mine_r = (x * 4 + y) * part
    own_r = pl.ds(pl.multiple_of(mine_r, part), part)
    own_r2 = pl.ds(pl.multiple_of(mid + mine_r, part), part)

    def scale(k):
        total = c_send[k, own_r].astype(f32)
        own_f = fs_ref[pl.ds(pl.multiple_of(k * width + z * LANES, LANES), LANES)][None, :]
        other_f = swap(jnp.broadcast_to(own_f, (8, LANES)))[:1]
        both = jnp.where(left == (core == 0), own_f, other_f)
        denom = jnp.where(left, tcol[own_r], tcol[own_r2]) + both + noise_var
        for q in reversed(PLANE_FAR_FIRST):
            cs[k, q].wait_recv()
            total = total + c_recv[k, q].astype(f32)
        scaled = (total / denom).astype(bf16)
        s_own[k] = scaled
        s_all[k, own_r] = scaled
        for q in PLANE_FAR_FIRST:
            ss[k, q] = send(s_own.at[k], s_all.at[k, own_r], s_ssem.at[k, q], s_rsem.at[k, q], plane(q))

    def mm3(k):
        for q in reversed(PLANE_FAR_FIRST):
            ss[k, q].wait_recv()
        for g in range(2):
            first = jnp.dot(t2[g, :, :mid], s_all[k], preferred_element_type=f32)
            second = jnp.dot(t2[g, :, mid:], s_all[k], preferred_element_type=f32)
            both = jnp.where(left, first, second)
            both = both + swap(both)
            m_send[k, g] = jnp.where(left, both[:half], both[half:]).astype(bf16)
        for m in PAIR_ORDER[:-1]:
            for e in range(2):
                dest = in_pair(m, e)
                ms[k, m, e] = send(m_send.at[k, (dest // 4 + zh) % 2], m_all.at[k, PAIRS - m, odd, core],
                                   m_ssem.at[k, m, e], m_rsem.at[k, PAIRS - m, odd], ring(dest))
        ms[k, 0, 0] = send(m_send.at[k, 0], m_all.at[k, 0, odd, core],
                           m_ssem.at[k, 0, 0], m_rsem.at[k, 0, odd], ring(in_pair(0, 1 - odd)))
        m_all[k, 0, odd, core] = m_send[k, 0]

    def forward(k, m, e, wait=True):
        slot = m_all.at[k, m, e, core]
        if wait:
            sem = m_rsem.at[k, m, e]
            remote(slot, slot, sem, sem, sibling).wait_recv()
        fw[k, m, e if isinstance(e, int) else wait] = send(slot, slot, f_ssem.at[k, m, e], f_rsem.at[k, m, e], sibling)

    def forward_all(k):
        forward(k, 0, odd, wait=False)
        forward(k, 0, 1 - odd)
        for m in (1, 3, 2):
            for e in range(2):
                forward(k, m, e)

    def mm4(k):
        total = None
        for m in (0, 1, 3, 2):
            sides = []
            for e in range(2):
                slot = m_all.at[k, m, e, core]
                remote(slot, slot, f_ssem.at[k, m, e], f_rsem.at[k, m, e], sibling).wait_recv()
                first, second = m_all[k, m, e, 0].astype(f32), m_all[k, m, e, 1].astype(f32)
                sides.append(jnp.concatenate([jnp.where(left, first, swap(second)),
                                              jnp.where(left, swap(first), second)], axis=0).astype(bf16))
            block = jnp.concatenate(sides, axis=1)
            add = jnp.dot(block, featst[k, m], preferred_element_type=f32)
            total = add if total is None else total + add
        if k == 0:
            acc[...] = total
        else:
            out[...] = (acc[...] + total).astype(out.dtype)

    def turn(k):
        for m in range(PAIRS):
            featst[k, m] = feats[k, m].T

    mm2(0)
    mm2(1)
    turn(0)
    scale(0)
    scale(1)
    turn(1)
    mm3(0)
    mm3(1)
    forward_all(0)
    mm4(0)
    forward_all(1)
    mm4(1)

    @pl.when(near)
    def _():
        for copy in t_out + t_on:
            copy.wait_send()

    for copy in t_sib:
        copy.wait_send()
    for key, copy in zs.items():
        if key[0] == CHUNKS - 1:
            copy.wait_send()
    for copies in (cx, cs, ss, ms, fw):
        for copy in copies.values():
            copy.wait_send()


def per_device(fields, basis, features, time_spectrum, feature_spectrum):
    rows, sites = fields.shape
    half = rows // 2
    n_basis = basis.shape[1]
    mid = n_basis // 2
    part = mid // PLANE
    any_space = pl.BlockSpec(memory_space=pl.ANY)
    dma = pltpu.SemaphoreType.DMA
    return pl.pallas_call(
        kernel,
        out_shape=jax.ShapeDtypeStruct((rows, sites), bf16),
        in_specs=[any_space] * 5,
        out_specs=pl.BlockSpec(memory_space=pltpu.VMEM),
        scratch_shapes=[
            pltpu.VMEM(time_spectrum.shape, f32),
            pltpu.VMEM(feature_spectrum.shape, f32),
            pltpu.VMEM((CHUNKS, PAIRS, sites, 256), bf16),
            pltpu.VMEM((CHUNKS, PAIRS, 256, sites), bf16),
            pltpu.VMEM((rows, sites), bf16),
            pltpu.VMEM((2, rows, n_basis), bf16),
            pltpu.VMEM((2, n_basis, rows), bf16),
            pltpu.VMEM((n_basis, LANES), f32),
            pltpu.VMEM((rows, sites), f32),
            pltpu.VMEM((CHUNKS, PAIRS, 2, half, LANES), f32),
            pltpu.VMEM((CHUNKS, PAIRS, 2, half, LANES), f32),
            pltpu.VMEM((CHUNKS, PAIRS, 2, half, LANES), f32),
            pltpu.VMEM((CHUNKS, PAIRS, 2, half, LANES), bf16),
            pltpu.VMEM((CHUNKS, RING, half, LANES), bf16),
            pltpu.VMEM((CHUNKS, mid, LANES), bf16),
            pltpu.VMEM((CHUNKS, PLANE, part, LANES), bf16),
            pltpu.VMEM((CHUNKS, part, LANES), bf16),
            pltpu.VMEM((CHUNKS, mid, LANES), bf16),
            pltpu.VMEM((CHUNKS, 2, half, LANES), bf16),
            pltpu.VMEM((CHUNKS, PAIRS, 2, 2, half, LANES), bf16),
            dma((4,)), dma((CHUNKS, PAIRS)),
            dma((2, 2)), dma((2,)), dma((2,)), dma((2,)),
            dma((CHUNKS, PAIRS)), dma((CHUNKS, PAIRS)),
            dma((CHUNKS, PAIRS, 2)), dma((CHUNKS, PAIRS, 2)),
            dma((CHUNKS, PLANE)), dma((CHUNKS, PLANE)),
            dma((CHUNKS, PLANE)), dma((CHUNKS, PLANE)),
            dma((CHUNKS, PAIRS, 2)), dma((CHUNKS, PAIRS, 2)),
            dma((CHUNKS, PAIRS, 2)), dma((CHUNKS, PAIRS, 2)),
        ],
        compiler_params=pltpu.CompilerParams(
            collective_id=0, has_side_effects=True, vmem_limit_bytes=60 * 2**20),
        cost_estimate=pl.CostEstimate(flops=3_600_000_000, bytes_accessed=13_000_000, transcendentals=0),
        name="solve",
    )(fields, basis, features, time_spectrum, feature_spectrum)


def solution(mesh):
    in_specs = (P("hour", "site"), P("hour", None), P("site", None), P(), P())
    out_specs = P("hour", "site")
    return jax.shard_map(
        per_device, mesh=mesh, in_specs=in_specs, out_specs=out_specs, check_vma=False
    )
```

```python
import functools

import jax
import jax.numpy as jnp
from jax import lax
from jax.experimental import pallas as pl
from jax.experimental.pallas import tpu as pltpu
from jax.sharding import PartitionSpec as P

noise_var = 0.1

RING = 8
PAIRS = 4
PLANE = 16
CHUNKS = 2
PIECES = 4
SKEW = 2
LANES = 128
PAIR_ORDER = (2, 1, 3, 0)
PLANE_FAR_FIRST = (10, 6, 14, 9, 11, 2, 8, 5, 7, 13, 15, 1, 3, 4, 12)
f32 = jnp.float32
bf16 = jnp.bfloat16


def kernel(fields, basis, features, ts_hbm, fs_hbm, out,
           ts_ref, fs_ref, feats, featst, fbuf, t2, tcol, acc,
           cx_own, cx_send, cx_recv, zs_send, zs_recv,
           c_send, c_recv, s_own, s_all, m_send, m_all,
           load_sem, feat_sem, t_ssem, t_rsem, u_ssem, u_rsem, cx_ssem, cx_rsem,
           zs_ssem, zs_rsem, c_ssem, c_rsem, s_ssem, s_rsem, m_ssem, m_rsem, f_ssem, f_rsem):
    hour, site = lax.axis_index("hour"), lax.axis_index("site")
    zh, x, y = hour >> 4, (hour >> 2) & 3, hour & 3
    zl, core = site >> 1, site & 1
    z = zh * 4 + zl
    odd = z & 1
    rows = fields.shape[0]
    half = rows // 2
    n_basis = basis.shape[1]
    mid = n_basis // 2
    width = features.shape[1] // CHUNKS
    part = mid // PLANE
    left = lax.broadcasted_iota(jnp.int32, (1, LANES), 1) < LANES // 2

    def at(z_, x_, y_, c_):
        return ((z_ >> 2) * 16 + x_ * 4 + y_, (z_ & 3) * 2 + c_)

    def ring(z_):
        return at(z_, x, y, core)

    def plane(q):
        return at(z, (x + q // 4) & 3, (y + q % 4) & 3, core)

    def in_pair(m, e):
        return (((z >> 1) + m) & 3) * 2 + e

    sibling = at(z, x, y, 1 - core)

    def remote(src, dst, ssem, rsem, device):
        return pltpu.make_async_remote_copy(
            src_ref=src, dst_ref=dst, send_sem=ssem, recv_sem=rsem,
            device_id=device, device_id_type=pl.DeviceIdType.MESH)

    def send(*args):
        copy = remote(*args)
        copy.start()
        return copy

    def swap(v):
        return pltpu.roll(v, LANES // 2, axis=1)

    load_f = pltpu.make_async_copy(fields, fbuf, load_sem.at[0])
    load_f.start()
    load_ts = pltpu.make_async_copy(ts_hbm, ts_ref, load_sem.at[2])
    load_ts.start()
    load_fs = pltpu.make_async_copy(fs_hbm, fs_ref, load_sem.at[3])
    load_fs.start()
    loads = {}
    for k in range(CHUNKS):
        for m in PAIR_ORDER:
            if (k, m) == (0, PAIR_ORDER[1]):
                barrier = pltpu.get_barrier_semaphore()
                for d in range(1, RING):
                    pl.semaphore_signal(barrier, inc=1, device_id=ring((z + d) & 7), device_id_type=pl.DeviceIdType.MESH)
                for q in range(1, PLANE):
                    pl.semaphore_signal(barrier, inc=1, device_id=plane(q), device_id_type=pl.DeviceIdType.MESH)
                pl.semaphore_signal(barrier, inc=1, device_id=sibling, device_id_type=pl.DeviceIdType.MESH)
            col = pl.multiple_of(k * width + (((z >> 1) + m) & 3) * 256, 256)
            loads[k, m] = pltpu.make_async_copy(
                features.at[:, pl.ds(col, 256)], feats.at[k, m], feat_sem.at[k, m])
            loads[k, m].start()

    load_t = pltpu.make_async_copy(basis, t2.at[0], load_sem.at[1])
    load_t.start()
    pl.semaphore_wait(barrier, RING - 1 + PLANE - 1 + 1)

    near = (zl == 0) | (zl == 3)
    edge = jnp.where(zl == 0, RING - 1, 1)
    edge_dev = ring((z + edge) & 7)
    inner_dev = ring((z + RING - edge) & 7)
    my_half = pl.ds(pl.multiple_of(core * half, half), half)
    t_out, t_on, t_sib = [], [], []
    for i in range(PIECES):
        piece = pl.ds(i * (n_basis // PIECES), n_basis // PIECES)
        mine, other = basis.at[my_half, piece], t2.at[1, my_half, piece]
        t_out.append(remote(mine, other, t_ssem.at[0, i], t_rsem.at[i], edge_dev))
        t_on.append(remote(other, other, t_ssem.at[1, i], t_rsem.at[i], inner_dev))
        t_sib.append(remote(other, other, u_ssem.at[i], u_rsem.at[i], sibling))

    @pl.when(near)
    def _():
        for copy in t_out:
            copy.start()

    load_ts.wait()
    load_fs.wait()
    tcol[...] = jnp.broadcast_to(ts_ref[...][None, :], (LANES, n_basis)).T

    load_f.wait()
    cx, zs = {}, {}

    def mm1(k, m):
        loads[k, m].wait()
        block = jnp.dot(fbuf[...], feats[k, m], preferred_element_type=f32)
        for e in range(2):
            top, low = block[:half, e * LANES:(e + 1) * LANES], block[half:, e * LANES:(e + 1) * LANES]
            first = jnp.where(left, top, swap(low))
            second = jnp.where(left, swap(top), low)
            cx_own[k, m, e] = jnp.where(core == 0, first, second)
            cx_send[k, m, e] = jnp.where(core == 0, second, first)
        cx[k, m] = send(cx_send.at[k, m], cx_recv.at[k, m], cx_ssem.at[k, m], cx_rsem.at[k, m], sibling)

    def pass_on(k, m):
        cx[k, m].wait_recv()
        if m:
            for e in range(2):
                zs_send[k, m, e] = (cx_own[k, m, e] + cx_recv[k, m, e]).astype(bf16)
                zs[k, m, e] = send(zs_send.at[k, m, e], zs_recv.at[k, z], zs_ssem.at[k, m, e],
                                   zs_rsem.at[k, PAIRS - m, odd], ring(in_pair(m, e)))
        else:
            zs_send[k, 0, 0] = (cx_own[k, 0, 1 - odd] + cx_recv[k, 0, 1 - odd]).astype(bf16)
            zs[k, 0, 0] = send(zs_send.at[k, 0, 0], zs_recv.at[k, z], zs_ssem.at[k, 0, 0],
                               zs_rsem.at[k, 0, odd], ring(in_pair(0, 1 - odd)))
            zs_recv[k, z] = (cx_own[k, 0, odd] + cx_recv[k, 0, odd]).astype(bf16)

    def t_pass(i):
        t_out[i].wait_recv()
        t_on[i].start()
        t_sib[i].start()

    blocks = [(k, m) for k in range(CHUNKS) for m in PAIR_ORDER]
    for i in range(len(blocks)):
        mm1(*blocks[i])
        if SKEW <= i < SKEW + PAIRS:
            pass_on(*blocks[i - SKEW])
        if i >= SKEW + PAIRS:
            pl.when(near)(functools.partial(t_pass, i - SKEW - PAIRS))

    @pl.when(near)
    def _():
        for i in range(len(blocks) - SKEW - PAIRS, PIECES):
            t_pass(i)

    for key, copy in zs.items():
        copy.wait_send()
    sent = set(zs)
    for m in PAIR_ORDER:
        pass_on(1, m)

    @pl.when(jnp.logical_not(near))
    def _():
        for i in range(PIECES):
            t_out[i].wait_recv()
            t_sib[i].start()

    load_t.wait()
    for i in range(PIECES):
        t_sib[i].wait_recv()

    cs, ss, ms, fw = {}, {}, {}, {}

    def wait_ring(k, sem, src, dst):
        for m in range(PAIRS):
            for e in range(2):
                if m:
                    remote(src, dst, sem.at[k, m, e], sem.at[k, m, e], sibling).wait_recv()
        other = sem.at[k, 0, 1 - odd]
        remote(src, dst, other, other, sibling).wait_recv()

    def mm2(k):
        wait_ring(k, zs_rsem, zs_send.at[k, 0, 0], zs_recv.at[k, 0])
        total = None
        for g in range(2):
            base = (zh if g == 0 else 1 - zh) * 4
            packed = ((zs_recv[k, base].astype(f32) + zs_recv[k, base + 1].astype(f32))
                      + (zs_recv[k, base + 2].astype(f32) + zs_recv[k, base + 3].astype(f32)))
            swapped = swap(packed)
            low = jnp.concatenate([jnp.where(left, packed, 0), jnp.where(left, swapped, 0)], axis=0).astype(bf16)
            high = jnp.concatenate([jnp.where(left, 0, swapped), jnp.where(left, 0, packed)], axis=0).astype(bf16)
            contract = (((0,), (0,)), ((), ()))
            add = (lax.dot_general(t2[g, :, :mid], low, contract, preferred_element_type=f32)
                   + lax.dot_general(t2[g, :, mid:], high, contract, preferred_element_type=f32))
            total = add if total is None else total + add
        c_send[k] = total.astype(bf16)
        for q in PLANE_FAR_FIRST:
            target = ((x + q // 4) & 3) * 4 + ((y + q % 4) & 3)
            src = c_send.at[k, pl.ds(pl.multiple_of(target * part, part), part)]
            cs[k, q] = send(src, c_recv.at[k, q], c_ssem.at[k, q], c_rsem.at[k, q], plane(q))

    mine_r = (x * 4 + y) * part
    own_r = pl.ds(pl.multiple_of(mine_r, part), part)
    own_r2 = pl.ds(pl.multiple_of(mid + mine_r, part), part)

    def scale(k):
        total = c_send[k, own_r].astype(f32)
        own_f = fs_ref[pl.ds(pl.multiple_of(k * width + z * LANES, LANES), LANES)][None, :]
        other_f = swap(jnp.broadcast_to(own_f, (8, LANES)))[:1]
        both = jnp.where(left == (core == 0), own_f, other_f)
        denom = jnp.where(left, tcol[own_r], tcol[own_r2]) + both + noise_var
        for q in reversed(PLANE_FAR_FIRST):
            cs[k, q].wait_recv()
            total = total + c_recv[k, q].astype(f32)
        scaled = (total / denom).astype(bf16)
        s_own[k] = scaled
        s_all[k, own_r] = scaled
        for q in PLANE_FAR_FIRST:
            ss[k, q] = send(s_own.at[k], s_all.at[k, own_r], s_ssem.at[k, q], s_rsem.at[k, q], plane(q))

    def mm3(k):
        for q in reversed(PLANE_FAR_FIRST):
            ss[k, q].wait_recv()
        for g in range(2):
            first = jnp.dot(t2[g, :, :mid], s_all[k], preferred_element_type=f32)
            second = jnp.dot(t2[g, :, mid:], s_all[k], preferred_element_type=f32)
            both = jnp.where(left, first, second)
            both = both + swap(both)
            m_send[k, g] = jnp.where(left, both[:half], both[half:]).astype(bf16)
        for m in PAIR_ORDER[:-1]:
            for e in range(2):
                dest = in_pair(m, e)
                ms[k, m, e] = send(m_send.at[k, (dest >> 2) ^ zh], m_all.at[k, PAIRS - m, odd, core],
                                   m_ssem.at[k, m, e], m_rsem.at[k, PAIRS - m, odd], ring(dest))
        ms[k, 0, 0] = send(m_send.at[k, 0], m_all.at[k, 0, odd, core],
                           m_ssem.at[k, 0, 0], m_rsem.at[k, 0, odd], ring(in_pair(0, 1 - odd)))
        m_all[k, 0, odd, core] = m_send[k, 0]

    def forward(k, m, e, wait=True):
        slot = m_all.at[k, m, e, core]
        if wait:
            sem = m_rsem.at[k, m, e]
            remote(slot, slot, sem, sem, sibling).wait_recv()
        fw[k, m, e if isinstance(e, int) else wait] = send(slot, slot, f_ssem.at[k, m, e], f_rsem.at[k, m, e], sibling)

    def forward_all(k):
        forward(k, 0, odd, wait=False)
        forward(k, 0, 1 - odd)
        for m in (1, 3, 2):
            for e in range(2):
                forward(k, m, e)

    def mm4(k):
        total = None
        for m in (0, 1, 3, 2):
            sides = []
            for e in range(2):
                slot = m_all.at[k, m, e, core]
                remote(slot, slot, f_ssem.at[k, m, e], f_rsem.at[k, m, e], sibling).wait_recv()
                first, second = m_all[k, m, e, 0].astype(f32), m_all[k, m, e, 1].astype(f32)
                sides.append(jnp.concatenate([jnp.where(left, first, swap(second)),
                                              jnp.where(left, swap(first), second)], axis=0).astype(bf16))
            block = jnp.concatenate(sides, axis=1)
            add = jnp.dot(block, featst[k, m], preferred_element_type=f32)
            total = add if total is None else total + add
        if k == 0:
            acc[...] = total
        else:
            out[...] = (acc[...] + total).astype(out.dtype)

    def turn(k):
        for m in range(PAIRS):
            featst[k, m] = feats[k, m].T

    mm2(0)
    mm2(1)
    turn(0)
    scale(0)
    scale(1)
    turn(1)
    mm3(0)
    mm3(1)
    forward_all(0)
    mm4(0)
    forward_all(1)
    mm4(1)

    @pl.when(near)
    def _():
        for copy in t_out + t_on:
            copy.wait_send()

    for copy in t_sib:
        copy.wait_send()
    for key, copy in zs.items():
        if key not in sent:
            copy.wait_send()
    for copies in (cx, cs, ss, ms, fw):
        for copy in copies.values():
            copy.wait_send()


def per_device(fields, basis, features, time_spectrum, feature_spectrum):
    rows, sites = fields.shape
    half = rows // 2
    n_basis = basis.shape[1]
    mid = n_basis // 2
    part = mid // PLANE
    any_space = pl.BlockSpec(memory_space=pl.ANY)
    dma = pltpu.SemaphoreType.DMA
    return pl.pallas_call(
        kernel,
        out_shape=pltpu.VMEM((rows, sites), bf16),
        in_specs=[any_space] * 5,
        out_specs=pl.BlockSpec(memory_space=pltpu.VMEM),
        scratch_shapes=[
            pltpu.VMEM(time_spectrum.shape, f32),
            pltpu.VMEM(feature_spectrum.shape, f32),
            pltpu.VMEM((CHUNKS, PAIRS, sites, 256), bf16),
            pltpu.VMEM((CHUNKS, PAIRS, 256, sites), bf16),
            pltpu.VMEM((rows, sites), bf16),
            pltpu.VMEM((2, rows, n_basis), bf16),
            pltpu.VMEM((n_basis, LANES), f32),
            pltpu.VMEM((rows, sites), f32),
            pltpu.VMEM((CHUNKS, PAIRS, 2, half, LANES), f32),
            pltpu.VMEM((CHUNKS, PAIRS, 2, half, LANES), f32),
            pltpu.VMEM((CHUNKS, PAIRS, 2, half, LANES), f32),
            pltpu.VMEM((CHUNKS, PAIRS, 2, half, LANES), bf16),
            pltpu.VMEM((CHUNKS, RING, half, LANES), bf16),
            pltpu.VMEM((CHUNKS, mid, LANES), bf16),
            pltpu.VMEM((CHUNKS, PLANE, part, LANES), bf16),
            pltpu.VMEM((CHUNKS, part, LANES), bf16),
            pltpu.VMEM((CHUNKS, mid, LANES), bf16),
            pltpu.VMEM((CHUNKS, 2, half, LANES), bf16),
            pltpu.VMEM((CHUNKS, PAIRS, 2, 2, half, LANES), bf16),
            dma((4,)), dma((CHUNKS, PAIRS)),
            dma((2, PIECES)), dma((PIECES,)), dma((PIECES,)), dma((PIECES,)),
            dma((CHUNKS, PAIRS)), dma((CHUNKS, PAIRS)),
            dma((CHUNKS, PAIRS, 2)), dma((CHUNKS, PAIRS, 2)),
            dma((CHUNKS, PLANE)), dma((CHUNKS, PLANE)),
            dma((CHUNKS, PLANE)), dma((CHUNKS, PLANE)),
            dma((CHUNKS, PAIRS, 2)), dma((CHUNKS, PAIRS, 2)),
            dma((CHUNKS, PAIRS, 2)), dma((CHUNKS, PAIRS, 2)),
        ],
        compiler_params=pltpu.CompilerParams(
            collective_id=0, has_side_effects=True, vmem_limit_bytes=60 * 2**20),
        cost_estimate=pl.CostEstimate(flops=3_600_000_000, bytes_accessed=13_000_000, transcendentals=0),
        name="solve",
    )(fields, basis, features, time_spectrum, feature_spectrum)


def solution(mesh):
    in_specs = (P("hour", "site"), P("hour", None), P("site", None), P(), P())
    out_specs = P("hour", "site")
    return jax.shard_map(
        per_device, mesh=mesh, in_specs=in_specs, out_specs=out_specs, check_vma=False
    )
```

```python
import functools

import jax
import jax.numpy as jnp
from jax import lax
from jax.experimental import pallas as pl
from jax.experimental.pallas import tpu as pltpu
from jax.sharding import PartitionSpec as P

noise_var = 0.1

RING = 8
PAIRS = 4
PLANE = 16
PIECES = 4
LANES = 128
ORDER = (2, 1, 3, 0)
LINE_ORDER = (2, 3, 1, 0)
PLANE_FAR_FIRST = (10, 6, 14, 9, 11, 2, 8, 5, 7, 13, 15, 1, 3, 4, 12)
f32 = jnp.float32
bf16 = jnp.bfloat16


def kernel(fields, basis, features, ts_hbm, fs_hbm, out,
           ts_ref, fs_ref, feats, featst, fbuf, t2, tcol, acc,
           lx_own, lx_send, lx_recv, lz_send, lz_recv, lc_send, lc_recv, lp_send, lp_recv, ls_own, ls_all, lm_send, lm_all,
           cx_own, cx_send, cx_recv, zs_send, zs_recv, c_send, c_recv, s_own, s_all, m_send, m_all,
           load_sem, feat_sem, t_ssem, t_rsem, u_ssem, u_rsem,
           lx_ssem, lx_rsem, lz_ssem, lz_rsem, lc_ssem, lc_rsem, lp_ssem, lp_rsem, ls_ssem, ls_rsem, lm_ssem, lm_rsem,
           lf_ssem, lf_rsem,
           cx_ssem, cx_rsem, zs_ssem, zs_rsem, c_ssem, c_rsem, s_ssem, s_rsem, m_ssem, m_rsem, f_ssem, f_rsem):
    hour, site = lax.axis_index("hour"), lax.axis_index("site")
    zh, x, y = hour >> 4, (hour >> 2) & 3, hour & 3
    zl, core = site >> 1, site & 1
    z = zh * 4 + zl
    odd = z & 1
    rows = fields.shape[0]
    half = rows // 2
    n_basis = basis.shape[1]
    mid = n_basis // 2
    width = features.shape[1] // 2
    part = n_basis // PLANE
    small = mid // PLANE
    left = lax.broadcasted_iota(jnp.int32, (1, LANES), 1) < LANES // 2
    contract = (((0,), (0,)), ((), ()))

    def at(z_, x_, y_, c_):
        return ((z_ >> 2) * 16 + x_ * 4 + y_, (z_ & 3) * 2 + c_)

    def ring(z_):
        return at(z_, x, y, core)

    def line(m):
        return at(z ^ m, x, y, core)

    def plane(q):
        return at(z, (x + q // 4) & 3, (y + q % 4) & 3, core)

    def plane_index(q):
        return ((x + q // 4) & 3) * 4 + ((y + q % 4) & 3)

    def in_pair(m, e):
        return (((z >> 1) + m) & 3) * 2 + e

    sibling = at(z, x, y, 1 - core)

    def remote(src, dst, ssem, rsem, device):
        return pltpu.make_async_remote_copy(
            src_ref=src, dst_ref=dst, send_sem=ssem, recv_sem=rsem,
            device_id=device, device_id_type=pl.DeviceIdType.MESH)

    def send(*args):
        copy = remote(*args)
        copy.start()
        return copy

    def swap(v):
        return pltpu.roll(v, LANES // 2, axis=1)

    load_f = pltpu.make_async_copy(fields, fbuf, load_sem.at[0])
    load_f.start()
    blocks = [("line", m) for m in LINE_ORDER] + [("ring", m) for m in ORDER]
    loads = {}
    for i, (kind, m) in enumerate(blocks):
        if kind == "line":
            col, slot = (zl ^ m) * 256, 0
        else:
            col, slot = width + (((z >> 1) + m) & 3) * 256, 1
        loads[kind, m] = pltpu.make_async_copy(
            features.at[:, pl.ds(pl.multiple_of(col, 256), 256)], feats.at[slot, m], feat_sem.at[slot, m])
        loads[kind, m].start()
        if i == 0:
            barrier = pltpu.get_barrier_semaphore()
            for d in (4, 3, 5, 2, 6, 1, 7):
                pl.semaphore_signal(barrier, inc=1, device_id=ring((z + d) & 7), device_id_type=pl.DeviceIdType.MESH)
            for q in PLANE_FAR_FIRST:
                pl.semaphore_signal(barrier, inc=1, device_id=plane(q), device_id_type=pl.DeviceIdType.MESH)
            pl.semaphore_signal(barrier, inc=1, device_id=sibling, device_id_type=pl.DeviceIdType.MESH)
    load_t = pltpu.make_async_copy(basis, t2.at[0], load_sem.at[1])
    load_t.start()
    load_ts = pltpu.make_async_copy(ts_hbm, ts_ref, load_sem.at[2])
    load_ts.start()
    load_fs = pltpu.make_async_copy(fs_hbm, fs_ref, load_sem.at[3])
    load_fs.start()
    pl.semaphore_wait(barrier, RING - 1 + PLANE - 1 + 1)

    near = (zl == 0) | (zl == 3)
    edge = jnp.where(zl == 0, RING - 1, 1)
    edge_dev = ring((z + edge) & 7)
    inner_dev = ring((z + RING - edge) & 7)
    my_half = pl.ds(pl.multiple_of(core * half, half), half)
    t_out, t_on, t_sib = [], [], []
    for i in range(PIECES):
        piece = pl.ds(i * (n_basis // PIECES), n_basis // PIECES)
        mine, other = basis.at[my_half, piece], t2.at[1, my_half, piece]
        t_out.append(remote(mine, other, t_ssem.at[0, i], t_rsem.at[i], edge_dev))
        t_on.append(remote(other, other, t_ssem.at[1, i], t_rsem.at[i], inner_dev))
        t_sib.append(remote(other, other, u_ssem.at[i], u_rsem.at[i], sibling))

    @pl.when(near)
    def _():
        for copy in t_out:
            copy.start()

    def t_pass(i):
        t_out[i].wait_recv()
        t_on[i].start()
        t_sib[i].start()

    load_f.wait()
    lx, lz, cx, zs = {}, {}, {}, {}

    def product(kind, m):
        loads[kind, m].wait()
        return jnp.dot(fbuf[...], feats[0 if kind == "line" else 1, m], preferred_element_type=f32)

    def line_product(m):
        block = product("line", m)
        low, high = block[:, :LANES], block[:, LANES:]
        lx_own[m] = jnp.where(core == 0, low, high)
        lx_send[m] = jnp.where(core == 0, high, low)
        lx[m] = send(lx_send.at[m], lx_recv.at[m], lx_ssem.at[m], lx_rsem.at[m], sibling)

    def line_pass(m):
        lx[m].wait_recv()
        if m:
            lz_send[m] = (lx_own[m] + lx_recv[m]).astype(bf16)
            lz[m] = send(lz_send.at[m], lz_recv.at[m], lz_ssem.at[m], lz_rsem.at[m], line(m))

    def ring_product(m):
        block = product("ring", m)
        for e in range(2):
            top, low = block[:half, e * LANES:(e + 1) * LANES], block[half:, e * LANES:(e + 1) * LANES]
            first = jnp.where(left, top, swap(low))
            second = jnp.where(left, swap(top), low)
            cx_own[m, e] = jnp.where(core == 0, first, second)
            cx_send[m, e] = jnp.where(core == 0, second, first)
        cx[m] = send(cx_send.at[m], cx_recv.at[m], cx_ssem.at[m], cx_rsem.at[m], sibling)

    def ring_pass(m):
        cx[m].wait_recv()
        if m:
            for e in range(2):
                zs_send[m, e] = (cx_own[m, e] + cx_recv[m, e]).astype(bf16)
                zs[m, e] = send(zs_send.at[m, e], zs_recv.at[z], zs_ssem.at[m, e],
                                zs_rsem.at[PAIRS - m, odd], ring(in_pair(m, e)))
        else:
            zs_send[0, 0] = (cx_own[0, 1 - odd] + cx_recv[0, 1 - odd]).astype(bf16)
            zs[0, 0] = send(zs_send.at[0, 0], zs_recv.at[z], zs_ssem.at[0, 0],
                            zs_rsem.at[0, odd], ring(in_pair(0, 1 - odd)))
            zs_recv[z] = (cx_own[0, odd] + cx_recv[0, odd]).astype(bf16)

    for m in LINE_ORDER[:2]:
        line_product(m)
    for i in range(2, PAIRS):
        line_product(LINE_ORDER[i])
        line_pass(LINE_ORDER[i - 2])
    for i in range(PAIRS):
        ring_product(ORDER[i])
        if i < 2:
            line_pass(LINE_ORDER[i + 2])
        else:
            pl.when(near)(functools.partial(t_pass, i - 2))

    @pl.when(near)
    def _():
        for i in range(2, PIECES):
            t_pass(i)

    for copy in lz.values():
        copy.wait_send()
    for m in ORDER:
        ring_pass(m)

    load_ts.wait()
    load_fs.wait()
    tcol[...] = jnp.broadcast_to(ts_ref[...][None, :], (LANES, n_basis)).T
    load_t.wait()

    lc, lp, ls, lm, lf = {}, {}, {}, {}, {}
    cs, ss, ms, fw = {}, {}, {}, {}
    mine_r = (x * 4 + y) * part
    own_r = pl.ds(pl.multiple_of(mine_r, part), part)
    small_r = (x * 4 + y) * small
    own_s = pl.ds(pl.multiple_of(small_r, small), small)
    own_s2 = pl.ds(pl.multiple_of(mid + small_r, small), small)

    def line_mm2():
        total = lx_own[0] + lx_recv[0]
        for m in reversed(LINE_ORDER[:-1]):
            lz[m].wait_recv()
            total = total + lz_recv[m].astype(f32)
        lc_send[...] = lax.dot_general(t2[0], total.astype(bf16), contract, preferred_element_type=f32).astype(bf16)
        for q in PLANE_FAR_FIRST:
            src = lc_send.at[pl.ds(pl.multiple_of(plane_index(q) * part, part), part)]
            lc[q] = send(src, lc_recv.at[q], lc_ssem.at[q], lc_rsem.at[q], plane(q))

    def line_trade():
        total = lc_send[own_r].astype(f32)
        for q in reversed(PLANE_FAR_FIRST):
            lc[q].wait_recv()
            total = total + lc_recv[q].astype(f32)
        lp_send[...] = total.astype(bf16)
        lp[0] = send(lp_send, lp_recv, lp_ssem.at[0], lp_rsem.at[0], ring(z ^ 4))
        return total

    def line_scale(total):
        own_f = fs_ref[pl.ds(pl.multiple_of(zl * 256 + core * LANES, LANES), LANES)][None, :]
        denom = tcol[own_r] + own_f + noise_var
        lp[0].wait_recv()
        scaled = ((total + lp_recv[...].astype(f32)) / denom).astype(bf16)
        ls_own[...] = scaled
        ls_all[own_r] = scaled
        for q in PLANE_FAR_FIRST:
            ls[q] = send(ls_own, ls_all.at[own_r], ls_ssem.at[q], ls_rsem.at[q], plane(q))

    def line_mm3():
        for q in reversed(PLANE_FAR_FIRST):
            ls[q].wait_recv()
        mixed = jnp.dot(t2[0], ls_all[...], preferred_element_type=f32).astype(bf16)
        lm_send[...] = mixed
        lm_all[0, core] = mixed
        for m in LINE_ORDER[:-1]:
            lm[m] = send(lm_send, lm_all.at[m, core], lm_ssem.at[m], lm_rsem.at[m], line(m))

    def line_forward():
        for m in reversed(LINE_ORDER):
            if m:
                lm[m].wait_recv()
            slot = lm_all.at[m, core]
            lf[m] = send(slot, slot, lf_ssem.at[m], lf_rsem.at[m], sibling)

    def line_mm4():
        total = None
        for m in reversed(LINE_ORDER):
            lf[m].wait_recv()
            block = jnp.concatenate([lm_all[m, 0], lm_all[m, 1]], axis=1)
            add = jnp.dot(block, featst[0, m], preferred_element_type=f32)
            total = add if total is None else total + add
        return total

    def wait_ring(sem, src, dst):
        for m in range(1, PAIRS):
            for e in range(2):
                remote(src, dst, sem.at[m, e], sem.at[m, e], sibling).wait_recv()
        other = sem.at[0, 1 - odd]
        remote(src, dst, other, other, sibling).wait_recv()

    def ring_mm2():
        wait_ring(zs_rsem, zs_send.at[0, 0], zs_recv.at[0])
        total = None
        for g in range(2):
            base = (zh if g == 0 else 1 - zh) * 4
            packed = ((zs_recv[base].astype(f32) + zs_recv[base + 1].astype(f32))
                      + (zs_recv[base + 2].astype(f32) + zs_recv[base + 3].astype(f32)))
            swapped = swap(packed)
            low = jnp.concatenate([jnp.where(left, packed, 0), jnp.where(left, swapped, 0)], axis=0).astype(bf16)
            high = jnp.concatenate([jnp.where(left, 0, swapped), jnp.where(left, 0, packed)], axis=0).astype(bf16)
            add = (lax.dot_general(t2[g, :, :mid], low, contract, preferred_element_type=f32)
                   + lax.dot_general(t2[g, :, mid:], high, contract, preferred_element_type=f32))
            total = add if total is None else total + add
        c_send[...] = total.astype(bf16)
        for q in PLANE_FAR_FIRST:
            src = c_send.at[pl.ds(pl.multiple_of(plane_index(q) * small, small), small)]
            cs[q] = send(src, c_recv.at[q], c_ssem.at[q], c_rsem.at[q], plane(q))

    def ring_scale():
        total = c_send[own_s].astype(f32)
        own_f = fs_ref[pl.ds(pl.multiple_of(width + z * LANES, LANES), LANES)][None, :]
        other_f = swap(jnp.broadcast_to(own_f, (8, LANES)))[:1]
        both = jnp.where(left == (core == 0), own_f, other_f)
        denom = jnp.where(left, tcol[own_s], tcol[own_s2]) + both + noise_var
        for q in reversed(PLANE_FAR_FIRST):
            cs[q].wait_recv()
            total = total + c_recv[q].astype(f32)
        scaled = (total / denom).astype(bf16)
        s_own[...] = scaled
        s_all[own_s] = scaled
        for q in PLANE_FAR_FIRST:
            ss[q] = send(s_own, s_all.at[own_s], s_ssem.at[q], s_rsem.at[q], plane(q))

    def ring_mm3():
        for q in reversed(PLANE_FAR_FIRST):
            ss[q].wait_recv()
        for g in range(2):
            first = jnp.dot(t2[g, :, :mid], s_all[...], preferred_element_type=f32)
            second = jnp.dot(t2[g, :, mid:], s_all[...], preferred_element_type=f32)
            both = jnp.where(left, first, second)
            both = both + swap(both)
            m_send[g] = jnp.where(left, both[:half], both[half:]).astype(bf16)
        for m in ORDER[:-1]:
            for e in range(2):
                dest = in_pair(m, e)
                ms[m, e] = send(m_send.at[(dest >> 2) ^ zh], m_all.at[PAIRS - m, odd, core],
                                m_ssem.at[m, e], m_rsem.at[PAIRS - m, odd], ring(dest))
        ms[0, 0] = send(m_send.at[0], m_all.at[0, odd, core],
                        m_ssem.at[0, 0], m_rsem.at[0, odd], ring(in_pair(0, 1 - odd)))
        m_all[0, odd, core] = m_send[0]

    def ring_forward():
        for m in (0, 1, 3, 2):
            for i in range(2):
                e = i ^ odd if m == 0 else i
                slot = m_all.at[m, e, core]
                if m or i:
                    sem = m_rsem.at[m, e]
                    remote(slot, slot, sem, sem, sibling).wait_recv()
                fw[m, i] = send(slot, slot, f_ssem.at[m, e], f_rsem.at[m, e], sibling)

    def ring_mm4():
        total = None
        for m in (0, 1, 3, 2):
            sides = []
            for e in range(2):
                slot = m_all.at[m, e, core]
                remote(slot, slot, f_ssem.at[m, e], f_rsem.at[m, e], sibling).wait_recv()
                first, second = m_all[m, e, 0].astype(f32), m_all[m, e, 1].astype(f32)
                sides.append(jnp.concatenate([jnp.where(left, first, swap(second)),
                                              jnp.where(left, swap(first), second)], axis=0).astype(bf16))
            block = jnp.concatenate(sides, axis=1)
            add = jnp.dot(block, featst[1, m], preferred_element_type=f32)
            total = add if total is None else total + add
        return total

    def turn(k):
        for m in range(PAIRS):
            featst[k, m] = feats[k, m].T

    line_mm2()

    @pl.when(jnp.logical_not(near))
    def _():
        for i in range(PIECES):
            t_out[i].wait_recv()
            t_sib[i].start()

    turn(0)
    line_sum = line_trade()
    for i in range(PIECES):
        t_sib[i].wait_recv()
    ring_mm2()
    line_scale(line_sum)
    turn(1)
    ring_scale()
    line_mm3()
    ring_mm3()
    line_forward()
    acc[...] = line_mm4()
    ring_forward()
    out[...] = (acc[...] + ring_mm4()).astype(out.dtype)

    @pl.when(near)
    def _():
        for copy in t_out + t_on:
            copy.wait_send()

    for copy in t_sib:
        copy.wait_send()
    for copies in (lx, lc, lp, ls, lm, lf, cx, zs, cs, ss, ms, fw):
        for copy in copies.values():
            copy.wait_send()


def per_device(fields, basis, features, time_spectrum, feature_spectrum):
    rows, sites = fields.shape
    half = rows // 2
    n_basis = basis.shape[1]
    mid = n_basis // 2
    part = n_basis // PLANE
    small = mid // PLANE
    any_space = pl.BlockSpec(memory_space=pl.ANY)
    vmem = pltpu.VMEM
    dma = pltpu.SemaphoreType.DMA
    return pl.pallas_call(
        kernel,
        out_shape=pltpu.VMEM((rows, sites), bf16),
        in_specs=[any_space] * 5,
        out_specs=pl.BlockSpec(memory_space=pltpu.VMEM),
        scratch_shapes=[
            vmem(time_spectrum.shape, f32),
            vmem(feature_spectrum.shape, f32),
            vmem((2, PAIRS, sites, 256), bf16),
            vmem((2, PAIRS, 256, sites), bf16),
            vmem((rows, sites), bf16),
            vmem((2, rows, n_basis), bf16),
            vmem((n_basis, LANES), f32),
            vmem((rows, sites), f32),
            vmem((PAIRS, rows, LANES), f32),
            vmem((PAIRS, rows, LANES), f32),
            vmem((PAIRS, rows, LANES), f32),
            vmem((PAIRS, rows, LANES), bf16),
            vmem((PAIRS, rows, LANES), bf16),
            vmem((n_basis, LANES), bf16),
            vmem((PLANE, part, LANES), bf16),
            vmem((part, LANES), bf16),
            vmem((part, LANES), bf16),
            vmem((part, LANES), bf16),
            vmem((n_basis, LANES), bf16),
            vmem((rows, LANES), bf16),
            vmem((PAIRS, 2, rows, LANES), bf16),
            vmem((PAIRS, 2, half, LANES), f32),
            vmem((PAIRS, 2, half, LANES), f32),
            vmem((PAIRS, 2, half, LANES), f32),
            vmem((PAIRS, 2, half, LANES), bf16),
            vmem((RING, half, LANES), bf16),
            vmem((mid, LANES), bf16),
            vmem((PLANE, small, LANES), bf16),
            vmem((small, LANES), bf16),
            vmem((mid, LANES), bf16),
            vmem((2, half, LANES), bf16),
            vmem((PAIRS, 2, 2, half, LANES), bf16),
            dma((4,)), dma((2, PAIRS)),
            dma((2, PIECES)), dma((PIECES,)), dma((PIECES,)), dma((PIECES,)),
            dma((PAIRS,)), dma((PAIRS,)), dma((PAIRS,)), dma((PAIRS,)),
            dma((PLANE,)), dma((PLANE,)), dma((1,)), dma((1,)), dma((PLANE,)), dma((PLANE,)),
            dma((PAIRS,)), dma((PAIRS,)), dma((PAIRS,)), dma((PAIRS,)),
            dma((PAIRS,)), dma((PAIRS,)), dma((PAIRS, 2)), dma((PAIRS, 2)),
            dma((PLANE,)), dma((PLANE,)), dma((PLANE,)), dma((PLANE,)),
            dma((PAIRS, 2)), dma((PAIRS, 2)), dma((PAIRS, 2)), dma((PAIRS, 2)),
        ],
        compiler_params=pltpu.CompilerParams(
            collective_id=0, has_side_effects=True, vmem_limit_bytes=60 * 2**20),
        cost_estimate=pl.CostEstimate(flops=3_600_000_000, bytes_accessed=13_000_000, transcendentals=0),
        name="solve",
    )(fields, basis, features, time_spectrum, feature_spectrum)


def solution(mesh):
    in_specs = (P("hour", "site"), P("hour", None), P("site", None), P(), P())
    out_specs = P("hour", "site")
    return jax.shard_map(
        per_device, mesh=mesh, in_specs=in_specs, out_specs=out_specs, check_vma=False
    )
```

```python
import functools

import jax
import jax.numpy as jnp
from jax import lax
from jax.experimental import pallas as pl
from jax.experimental.pallas import tpu as pltpu
from jax.sharding import PartitionSpec as P

noise_var = 0.1

RING = 8
PAIRS = 4
PLANE = 16
PIECES = 4
LANES = 128
ORDER = (2, 1, 3, 0)
LINE_ORDER = (2, 3, 1, 0)
PLANE_FAR_FIRST = (10, 6, 14, 9, 11, 2, 8, 5, 7, 13, 15, 1, 3, 4, 12)
f32 = jnp.float32
bf16 = jnp.bfloat16


def kernel(fields, basis, features, ts_hbm, fs_hbm, out,
           ts_ref, fs_ref, feats, featst, fbuf, t2, tcol, acc,
           lx_own, lx_send, lx_recv, lz_send, lz_recv, lc_send, lc_recv, lp_send, lp_recv, ls_own, ls_all, lm_send, lm_all,
           cx_own, cx_send, cx_recv, zs_send, zs_recv, c_send, c_recv, s_own, s_all, m_send, m_all,
           load_sem, feat_sem, t_ssem, t_rsem, u_ssem, u_rsem,
           lx_ssem, lx_rsem, lz_ssem, lz_rsem, lc_ssem, lc_rsem, lp_ssem, lp_rsem, ls_ssem, ls_rsem, lm_ssem, lm_rsem,
           lf_ssem, lf_rsem,
           cx_ssem, cx_rsem, zs_ssem, zs_rsem, c_ssem, c_rsem, s_ssem, s_rsem, m_ssem, m_rsem, f_ssem, f_rsem):
    hour, site = lax.axis_index("hour"), lax.axis_index("site")
    zh, x, y = hour >> 4, (hour >> 2) & 3, hour & 3
    zl, core = site >> 1, site & 1
    z = zh * 4 + zl
    odd = z & 1
    rows = fields.shape[0]
    half = rows // 2
    n_basis = basis.shape[1]
    mid = n_basis // 2
    width = features.shape[1] // 2
    part = n_basis // PLANE
    small = mid // PLANE
    left = lax.broadcasted_iota(jnp.int32, (1, LANES), 1) < LANES // 2
    contract = (((0,), (0,)), ((), ()))

    def at(z_, x_, y_, c_):
        return ((z_ >> 2) * 16 + x_ * 4 + y_, (z_ & 3) * 2 + c_)

    def ring(z_):
        return at(z_, x, y, core)

    def line(m):
        return at(z ^ m, x, y, core)

    def plane(q):
        return at(z, (x + q // 4) & 3, (y + q % 4) & 3, core)

    def plane_index(q):
        return ((x + q // 4) & 3) * 4 + ((y + q % 4) & 3)

    def in_pair(m, e):
        return (((z >> 1) + m) & 3) * 2 + e

    sibling = at(z, x, y, 1 - core)

    def remote(src, dst, ssem, rsem, device):
        return pltpu.make_async_remote_copy(
            src_ref=src, dst_ref=dst, send_sem=ssem, recv_sem=rsem,
            device_id=device, device_id_type=pl.DeviceIdType.MESH)

    def send(*args):
        copy = remote(*args)
        copy.start()
        return copy

    def swap(v):
        return pltpu.roll(v, LANES // 2, axis=1)

    load_f = pltpu.make_async_copy(fields, fbuf, load_sem.at[0])
    load_f.start()
    blocks = [("line", m) for m in LINE_ORDER] + [("ring", m) for m in ORDER]
    loads = {}
    for i, (kind, m) in enumerate(blocks):
        if kind == "line":
            col, slot = (zl ^ m) * 256, 0
        else:
            col, slot = width + (((z >> 1) + m) & 3) * 256, 1
        loads[kind, m] = pltpu.make_async_copy(
            features.at[:, pl.ds(pl.multiple_of(col, 256), 256)], feats.at[slot, m], feat_sem.at[slot, m])
        loads[kind, m].start()
        if i == 0:
            barrier = pltpu.get_barrier_semaphore()
            for d in (4, 3, 5, 2, 6, 1, 7):
                pl.semaphore_signal(barrier, inc=1, device_id=ring((z + d) & 7), device_id_type=pl.DeviceIdType.MESH)
            for q in PLANE_FAR_FIRST:
                pl.semaphore_signal(barrier, inc=1, device_id=plane(q), device_id_type=pl.DeviceIdType.MESH)
            pl.semaphore_signal(barrier, inc=1, device_id=sibling, device_id_type=pl.DeviceIdType.MESH)
    load_t = pltpu.make_async_copy(basis, t2.at[0], load_sem.at[1])
    load_t.start()
    load_ts = pltpu.make_async_copy(ts_hbm, ts_ref, load_sem.at[2])
    load_ts.start()
    load_fs = pltpu.make_async_copy(fs_hbm, fs_ref, load_sem.at[3])
    load_fs.start()
    near = (zl == 0) | (zl == 3)
    edge = jnp.where(zl == 0, RING - 1, 1)
    edge_dev = ring((z + edge) & 7)
    inner_dev = ring((z + RING - edge) & 7)
    my_half = pl.ds(pl.multiple_of(core * half, half), half)
    t_out, t_on, t_sib = [], [], []
    for i in range(PIECES):
        piece = pl.ds(i * (n_basis // PIECES), n_basis // PIECES)
        mine, other = basis.at[my_half, piece], t2.at[1, my_half, piece]
        t_out.append(remote(mine, other, t_ssem.at[0, i], t_rsem.at[i], edge_dev))
        t_on.append(remote(other, other, t_ssem.at[1, i], t_rsem.at[i], inner_dev))
        t_sib.append(remote(other, other, u_ssem.at[i], u_rsem.at[i], sibling))

    def t_pass(i):
        t_out[i].wait_recv()
        t_on[i].start()
        t_sib[i].start()

    load_f.wait()
    lx, lz, cx, zs = {}, {}, {}, {}

    def product(kind, m):
        loads[kind, m].wait()
        return jnp.dot(fbuf[...], feats[0 if kind == "line" else 1, m], preferred_element_type=f32)

    def line_product(m):
        block = product("line", m)
        low, high = block[:, :LANES], block[:, LANES:]
        lx_own[m] = jnp.where(core == 0, low, high)
        lx_send[m] = jnp.where(core == 0, high, low)

    def line_swap(m):
        lx[m] = send(lx_send.at[m], lx_recv.at[m], lx_ssem.at[m], lx_rsem.at[m], sibling)

    def line_pass(m):
        lx[m].wait_recv()
        if m:
            lz_send[m] = (lx_own[m] + lx_recv[m]).astype(bf16)
            lz[m] = send(lz_send.at[m], lz_recv.at[m], lz_ssem.at[m], lz_rsem.at[m], line(m))

    def ring_product(m):
        block = product("ring", m)
        for e in range(2):
            top, low = block[:half, e * LANES:(e + 1) * LANES], block[half:, e * LANES:(e + 1) * LANES]
            first = jnp.where(left, top, swap(low))
            second = jnp.where(left, swap(top), low)
            cx_own[m, e] = jnp.where(core == 0, first, second)
            cx_send[m, e] = jnp.where(core == 0, second, first)
        cx[m] = send(cx_send.at[m], cx_recv.at[m], cx_ssem.at[m], cx_rsem.at[m], sibling)

    def ring_pass(m):
        cx[m].wait_recv()
        if m:
            for e in range(2):
                zs_send[m, e] = (cx_own[m, e] + cx_recv[m, e]).astype(bf16)
                zs[m, e] = send(zs_send.at[m, e], zs_recv.at[z], zs_ssem.at[m, e],
                                zs_rsem.at[PAIRS - m, odd], ring(in_pair(m, e)))
        else:
            zs_send[0, 0] = (cx_own[0, 1 - odd] + cx_recv[0, 1 - odd]).astype(bf16)
            zs[0, 0] = send(zs_send.at[0, 0], zs_recv.at[z], zs_ssem.at[0, 0],
                            zs_rsem.at[0, odd], ring(in_pair(0, 1 - odd)))
            zs_recv[z] = (cx_own[0, odd] + cx_recv[0, odd]).astype(bf16)

    for m in LINE_ORDER[:1]:
        line_product(m)
    pl.semaphore_wait(barrier, RING - 1 + PLANE - 1 + 1)

    @pl.when(near)
    def _():
        for copy in t_out:
            copy.start()

    for m in LINE_ORDER[:1]:
        line_swap(m)
    line_product(LINE_ORDER[1])
    line_swap(LINE_ORDER[1])
    line_product(LINE_ORDER[2])
    line_swap(LINE_ORDER[2])
    line_pass(LINE_ORDER[0])
    line_product(LINE_ORDER[3])
    line_swap(LINE_ORDER[3])
    line_pass(LINE_ORDER[1])
    ring_product(ORDER[0])
    line_pass(LINE_ORDER[2])
    ring_product(ORDER[1])
    line_pass(LINE_ORDER[3])
    for i in range(2, PAIRS):
        ring_product(ORDER[i])
        pl.when(near)(functools.partial(t_pass, i - 2))

    @pl.when(near)
    def _():
        for i in range(2, PIECES):
            t_pass(i)

    for copy in lz.values():
        copy.wait_send()
    for m in ORDER:
        ring_pass(m)

    load_ts.wait()
    load_fs.wait()
    tcol[...] = jnp.broadcast_to(ts_ref[...][None, :], (LANES, n_basis)).T
    load_t.wait()

    lc, lp, ls, lm, lf = {}, {}, {}, {}, {}
    cs, ss, ms, fw = {}, {}, {}, {}
    mine_r = (x * 4 + y) * part
    own_r = pl.ds(pl.multiple_of(mine_r, part), part)
    small_r = (x * 4 + y) * small
    own_s = pl.ds(pl.multiple_of(small_r, small), small)
    own_s2 = pl.ds(pl.multiple_of(mid + small_r, small), small)

    def line_mm2():
        total = lx_own[0] + lx_recv[0]
        for m in reversed(LINE_ORDER[:-1]):
            lz[m].wait_recv()
            total = total + lz_recv[m].astype(f32)
        lc_send[...] = lax.dot_general(t2[0], total.astype(bf16), contract, preferred_element_type=f32).astype(bf16)
        for q in PLANE_FAR_FIRST:
            src = lc_send.at[pl.ds(pl.multiple_of(plane_index(q) * part, part), part)]
            lc[q] = send(src, lc_recv.at[q], lc_ssem.at[q], lc_rsem.at[q], plane(q))

    def line_trade():
        total = lc_send[own_r].astype(f32)
        for q in reversed(PLANE_FAR_FIRST):
            lc[q].wait_recv()
            total = total + lc_recv[q].astype(f32)
        lp_send[...] = total.astype(bf16)
        lp[0] = send(lp_send, lp_recv, lp_ssem.at[0], lp_rsem.at[0], ring(z ^ 4))
        return total

    def line_scale(total):
        own_f = fs_ref[pl.ds(pl.multiple_of(zl * 256 + core * LANES, LANES), LANES)][None, :]
        denom = tcol[own_r] + own_f + noise_var
        lp[0].wait_recv()
        scaled = ((total + lp_recv[...].astype(f32)) / denom).astype(bf16)
        ls_own[...] = scaled
        ls_all[own_r] = scaled
        for q in PLANE_FAR_FIRST:
            ls[q] = send(ls_own, ls_all.at[own_r], ls_ssem.at[q], ls_rsem.at[q], plane(q))

    def line_mm3():
        for q in reversed(PLANE_FAR_FIRST):
            ls[q].wait_recv()
        mixed = jnp.dot(t2[0], ls_all[...], preferred_element_type=f32).astype(bf16)
        lm_send[...] = mixed
        lm_all[0, core] = mixed
        for m in LINE_ORDER[:-1]:
            lm[m] = send(lm_send, lm_all.at[m, core], lm_ssem.at[m], lm_rsem.at[m], line(m))

    def line_forward(m):
        if m:
            lm[m].wait_recv()
        slot = lm_all.at[m, core]
        lf[m] = send(slot, slot, lf_ssem.at[m], lf_rsem.at[m], sibling)

    def line_mm4(m):
        lf[m].wait_recv()
        block = jnp.concatenate([lm_all[m, 0], lm_all[m, 1]], axis=1)
        return jnp.dot(block, featst[0, m], preferred_element_type=f32)

    def wait_ring(sem, src, dst):
        for m in range(1, PAIRS):
            for e in range(2):
                remote(src, dst, sem.at[m, e], sem.at[m, e], sibling).wait_recv()
        other = sem.at[0, 1 - odd]
        remote(src, dst, other, other, sibling).wait_recv()

    def ring_mm2():
        wait_ring(zs_rsem, zs_send.at[0, 0], zs_recv.at[0])
        total = None
        for g in range(2):
            base = (zh if g == 0 else 1 - zh) * 4
            packed = ((zs_recv[base].astype(f32) + zs_recv[base + 1].astype(f32))
                      + (zs_recv[base + 2].astype(f32) + zs_recv[base + 3].astype(f32)))
            swapped = swap(packed)
            low = jnp.concatenate([jnp.where(left, packed, 0), jnp.where(left, swapped, 0)], axis=0).astype(bf16)
            high = jnp.concatenate([jnp.where(left, 0, swapped), jnp.where(left, 0, packed)], axis=0).astype(bf16)
            add = (lax.dot_general(t2[g, :, :mid], low, contract, preferred_element_type=f32)
                   + lax.dot_general(t2[g, :, mid:], high, contract, preferred_element_type=f32))
            total = add if total is None else total + add
        c_send[...] = total.astype(bf16)
        for q in PLANE_FAR_FIRST:
            src = c_send.at[pl.ds(pl.multiple_of(plane_index(q) * small, small), small)]
            cs[q] = send(src, c_recv.at[q], c_ssem.at[q], c_rsem.at[q], plane(q))

    def ring_scale():
        total = c_send[own_s].astype(f32)
        own_f = fs_ref[pl.ds(pl.multiple_of(width + z * LANES, LANES), LANES)][None, :]
        other_f = swap(jnp.broadcast_to(own_f, (8, LANES)))[:1]
        both = jnp.where(left == (core == 0), own_f, other_f)
        denom = jnp.where(left, tcol[own_s], tcol[own_s2]) + both + noise_var
        for q in reversed(PLANE_FAR_FIRST):
            cs[q].wait_recv()
            total = total + c_recv[q].astype(f32)
        scaled = (total / denom).astype(bf16)
        s_own[...] = scaled
        s_all[own_s] = scaled
        for q in PLANE_FAR_FIRST:
            ss[q] = send(s_own, s_all.at[own_s], s_ssem.at[q], s_rsem.at[q], plane(q))

    def ring_mm3():
        for q in reversed(PLANE_FAR_FIRST):
            ss[q].wait_recv()
        for g in range(2):
            first = jnp.dot(t2[g, :, :mid], s_all[...], preferred_element_type=f32)
            second = jnp.dot(t2[g, :, mid:], s_all[...], preferred_element_type=f32)
            both = jnp.where(left, first, second)
            both = both + swap(both)
            m_send[g] = jnp.where(left, both[:half], both[half:]).astype(bf16)
        for m in ORDER[:-1]:
            for e in range(2):
                dest = in_pair(m, e)
                ms[m, e] = send(m_send.at[(dest >> 2) ^ zh], m_all.at[PAIRS - m, odd, core],
                                m_ssem.at[m, e], m_rsem.at[PAIRS - m, odd], ring(dest))
        ms[0, 0] = send(m_send.at[0], m_all.at[0, odd, core],
                        m_ssem.at[0, 0], m_rsem.at[0, odd], ring(in_pair(0, 1 - odd)))
        m_all[0, odd, core] = m_send[0]

    def ring_forward(m):
        for i in range(2):
            e = i ^ odd if m == 0 else i
            slot = m_all.at[m, e, core]
            if m or i:
                sem = m_rsem.at[m, e]
                remote(slot, slot, sem, sem, sibling).wait_recv()
            fw[m, i] = send(slot, slot, f_ssem.at[m, e], f_rsem.at[m, e], sibling)

    def ring_mm4(m):
        sides = []
        for e in range(2):
            slot = m_all.at[m, e, core]
            remote(slot, slot, f_ssem.at[m, e], f_rsem.at[m, e], sibling).wait_recv()
            first, second = m_all[m, e, 0].astype(f32), m_all[m, e, 1].astype(f32)
            sides.append(jnp.concatenate([jnp.where(left, first, swap(second)),
                                          jnp.where(left, swap(first), second)], axis=0).astype(bf16))
        return jnp.dot(jnp.concatenate(sides, axis=1), featst[1, m], preferred_element_type=f32)

    def turn(k):
        for m in range(PAIRS):
            featst[k, m] = feats[k, m].T

    line_mm2()

    @pl.when(jnp.logical_not(near))
    def _():
        for i in range(PIECES):
            t_out[i].wait_recv()
            t_sib[i].start()

    turn(0)
    line_sum = line_trade()
    for i in range(PIECES):
        t_sib[i].wait_recv()
    ring_mm2()
    line_scale(line_sum)
    turn(1)
    ring_scale()
    line_mm3()
    ring_mm3()
    last = [("line", m) for m in reversed(LINE_ORDER)] + [("ring", m) for m in (0, 1, 3, 2)]
    for i in range(len(last) + 1):
        if i < len(last):
            (line_forward if last[i][0] == "line" else ring_forward)(last[i][1])
        if i == 0:
            continue
        kind, m = last[i - 1]
        add = line_mm4(m) if kind == "line" else ring_mm4(m)
        if i == 1:
            acc[...] = add
        elif i < len(last):
            acc[...] += add
        else:
            out[...] = (acc[...] + add).astype(out.dtype)

    @pl.when(near)
    def _():
        for copy in t_out + t_on:
            copy.wait_send()

    for copy in t_sib:
        copy.wait_send()
    for copies in (lx, lc, lp, ls, lm, lf, cx, zs, cs, ss, ms, fw):
        for copy in copies.values():
            copy.wait_send()


def per_device(fields, basis, features, time_spectrum, feature_spectrum):
    rows, sites = fields.shape
    half = rows // 2
    n_basis = basis.shape[1]
    mid = n_basis // 2
    part = n_basis // PLANE
    small = mid // PLANE
    any_space = pl.BlockSpec(memory_space=pl.ANY)
    vmem = pltpu.VMEM
    dma = pltpu.SemaphoreType.DMA
    return pl.pallas_call(
        kernel,
        out_shape=pltpu.VMEM((rows, sites), bf16),
        in_specs=[any_space] * 5,
        out_specs=pl.BlockSpec(memory_space=pltpu.VMEM),
        scratch_shapes=[
            vmem(time_spectrum.shape, f32),
            vmem(feature_spectrum.shape, f32),
            vmem((2, PAIRS, sites, 256), bf16),
            vmem((2, PAIRS, 256, sites), bf16),
            vmem((rows, sites), bf16),
            vmem((2, rows, n_basis), bf16),
            vmem((n_basis, LANES), f32),
            vmem((rows, sites), f32),
            vmem((PAIRS, rows, LANES), f32),
            vmem((PAIRS, rows, LANES), f32),
            vmem((PAIRS, rows, LANES), f32),
            vmem((PAIRS, rows, LANES), bf16),
            vmem((PAIRS, rows, LANES), bf16),
            vmem((n_basis, LANES), bf16),
            vmem((PLANE, part, LANES), bf16),
            vmem((part, LANES), bf16),
            vmem((part, LANES), bf16),
            vmem((part, LANES), bf16),
            vmem((n_basis, LANES), bf16),
            vmem((rows, LANES), bf16),
            vmem((PAIRS, 2, rows, LANES), bf16),
            vmem((PAIRS, 2, half, LANES), f32),
            vmem((PAIRS, 2, half, LANES), f32),
            vmem((PAIRS, 2, half, LANES), f32),
            vmem((PAIRS, 2, half, LANES), bf16),
            vmem((RING, half, LANES), bf16),
            vmem((mid, LANES), bf16),
            vmem((PLANE, small, LANES), bf16),
            vmem((small, LANES), bf16),
            vmem((mid, LANES), bf16),
            vmem((2, half, LANES), bf16),
            vmem((PAIRS, 2, 2, half, LANES), bf16),
            dma((4,)), dma((2, PAIRS)),
            dma((2, PIECES)), dma((PIECES,)), dma((PIECES,)), dma((PIECES,)),
            dma((PAIRS,)), dma((PAIRS,)), dma((PAIRS,)), dma((PAIRS,)),
            dma((PLANE,)), dma((PLANE,)), dma((1,)), dma((1,)), dma((PLANE,)), dma((PLANE,)),
            dma((PAIRS,)), dma((PAIRS,)), dma((PAIRS,)), dma((PAIRS,)),
            dma((PAIRS,)), dma((PAIRS,)), dma((PAIRS, 2)), dma((PAIRS, 2)),
            dma((PLANE,)), dma((PLANE,)), dma((PLANE,)), dma((PLANE,)),
            dma((PAIRS, 2)), dma((PAIRS, 2)), dma((PAIRS, 2)), dma((PAIRS, 2)),
        ],
        compiler_params=pltpu.CompilerParams(
            collective_id=0, has_side_effects=True, vmem_limit_bytes=60 * 2**20),
        cost_estimate=pl.CostEstimate(flops=3_600_000_000, bytes_accessed=13_000_000, transcendentals=0),
        name="solve",
    )(fields, basis, features, time_spectrum, feature_spectrum)


def solution(mesh):
    in_specs = (P("hour", "site"), P("hour", None), P("site", None), P(), P())
    out_specs = P("hour", "site")
    return jax.shard_map(
        per_device, mesh=mesh, in_specs=in_specs, out_specs=out_specs, check_vma=False
    )
```

```python
import functools

import jax
import jax.numpy as jnp
from jax import lax
from jax.experimental import pallas as pl
from jax.experimental.pallas import tpu as pltpu
from jax.sharding import PartitionSpec as P

noise_var = 0.1

RING = 8
PAIRS = 4
PLANE = 16
PIECES = 4
LANES = 128
ORDER = (2, 1, 3, 0)
LINE_ORDER = (2, 3, 1, 0)
PLANE_FAR_FIRST = (10, 6, 14, 9, 11, 2, 8, 5, 7, 13, 15, 1, 3, 4, 12)
f32 = jnp.float32
bf16 = jnp.bfloat16


def kernel(fields, basis, features, ts_hbm, fs_hbm, out,
           ts_ref, fs_ref, feats, featst, fbuf, t2, tcol, acc,
           lx_own, lx_send, lx_recv, lz_send, lz_recv, lc_send, lc_recv, lp_send, lp_recv, ls_own, ls_all, lm_send, lm_all,
           cx_own, cx_send, cx_recv, zs_send, zs_recv, c_send, c_recv, s_own, s_all, m_send, m_all,
           load_sem, feat_sem, t_ssem, t_rsem, u_ssem, u_rsem,
           lx_ssem, lx_rsem, lz_ssem, lz_rsem, lc_ssem, lc_rsem, lp_ssem, lp_rsem, ls_ssem, ls_rsem, lm_ssem, lm_rsem,
           lf_ssem, lf_rsem,
           cx_ssem, cx_rsem, zs_ssem, zs_rsem, c_ssem, c_rsem, s_ssem, s_rsem, m_ssem, m_rsem, f_ssem, f_rsem):
    hour, site = lax.axis_index("hour"), lax.axis_index("site")
    zh, x, y = hour >> 4, (hour >> 2) & 3, hour & 3
    zl, core = site >> 1, site & 1
    z = zh * 4 + zl
    odd = z & 1
    owner = zl ^ (3 * zh)
    rows = fields.shape[0]
    half = rows // 2
    n_basis = basis.shape[1]
    mid = n_basis // 2
    width = features.shape[1] // 2
    part = n_basis // PLANE
    small = mid // PLANE
    left = lax.broadcasted_iota(jnp.int32, (1, LANES), 1) < LANES // 2
    contract = (((0,), (0,)), ((), ()))

    def at(z_, x_, y_, c_):
        return ((z_ >> 2) * 16 + x_ * 4 + y_, (z_ & 3) * 2 + c_)

    def ring(z_):
        return at(z_, x, y, core)

    def line(m):
        return at(z ^ m, x, y, core)

    def plane(q):
        return at(z, (x + q // 4) & 3, (y + q % 4) & 3, core)

    def plane_index(q):
        return ((x + q // 4) & 3) * 4 + ((y + q % 4) & 3)

    def in_pair(m, e):
        return (((z >> 1) + m) & 3) * 2 + e

    sibling = at(z, x, y, 1 - core)

    def remote(src, dst, ssem, rsem, device):
        return pltpu.make_async_remote_copy(
            src_ref=src, dst_ref=dst, send_sem=ssem, recv_sem=rsem,
            device_id=device, device_id_type=pl.DeviceIdType.MESH)

    def send(*args):
        copy = remote(*args)
        copy.start()
        return copy

    def swap(v):
        return pltpu.roll(v, LANES // 2, axis=1)

    load_f = pltpu.make_async_copy(fields, fbuf, load_sem.at[0])
    load_f.start()
    blocks = [("line", m) for m in LINE_ORDER] + [("ring", m) for m in ORDER]
    loads = {}
    for i, (kind, m) in enumerate(blocks):
        if kind == "line":
            col, slot = (owner ^ m) * 256, 0
        else:
            col, slot = width + (((z >> 1) + m) & 3) * 256, 1
        loads[kind, m] = pltpu.make_async_copy(
            features.at[:, pl.ds(pl.multiple_of(col, 256), 256)], feats.at[slot, m], feat_sem.at[slot, m])
        loads[kind, m].start()
        if i == 0:
            barrier = pltpu.get_barrier_semaphore()
            for d in (4, 3, 5, 2, 6, 1, 7):
                pl.semaphore_signal(barrier, inc=1, device_id=ring((z + d) & 7), device_id_type=pl.DeviceIdType.MESH)
            for q in PLANE_FAR_FIRST:
                pl.semaphore_signal(barrier, inc=1, device_id=plane(q), device_id_type=pl.DeviceIdType.MESH)
            pl.semaphore_signal(barrier, inc=1, device_id=sibling, device_id_type=pl.DeviceIdType.MESH)
    load_t = pltpu.make_async_copy(basis, t2.at[0], load_sem.at[1])
    load_t.start()
    load_ts = pltpu.make_async_copy(ts_hbm, ts_ref, load_sem.at[2])
    load_ts.start()
    load_fs = pltpu.make_async_copy(fs_hbm, fs_ref, load_sem.at[3])
    load_fs.start()
    near = (zl == 0) | (zl == 3)
    edge = jnp.where(zl == 0, RING - 1, 1)
    edge_dev = ring((z + edge) & 7)
    inner_dev = ring((z + RING - edge) & 7)
    my_half = pl.ds(pl.multiple_of(core * half, half), half)
    t_out, t_on, t_sib = [], [], []
    for i in range(PIECES):
        piece = pl.ds(i * (n_basis // PIECES), n_basis // PIECES)
        mine, other = basis.at[my_half, piece], t2.at[1, my_half, piece]
        t_out.append(remote(mine, other, t_ssem.at[0, i], t_rsem.at[i], edge_dev))
        t_on.append(remote(other, other, t_ssem.at[1, i], t_rsem.at[i], inner_dev))
        t_sib.append(remote(other, other, u_ssem.at[i], u_rsem.at[i], sibling))

    def t_pass(i):
        t_out[i].wait_recv()
        t_on[i].start()
        t_sib[i].start()

    load_f.wait()
    lx, lz, cx, zs = {}, {}, {}, {}

    def product(kind, m):
        loads[kind, m].wait()
        return jnp.dot(fbuf[...], feats[0 if kind == "line" else 1, m], preferred_element_type=f32)

    def line_product(m):
        block = product("line", m)
        low, high = block[:, :LANES], block[:, LANES:]
        lx_own[m] = jnp.where(core == 0, low, high)
        lx_send[m] = jnp.where(core == 0, high, low)

    def line_swap(m):
        lx[m] = send(lx_send.at[m], lx_recv.at[m], lx_ssem.at[m], lx_rsem.at[m], sibling)

    def line_pass(m):
        lx[m].wait_recv()
        if m:
            lz_send[m] = (lx_own[m] + lx_recv[m]).astype(bf16)
            lz[m] = send(lz_send.at[m], lz_recv.at[m], lz_ssem.at[m], lz_rsem.at[m], line(m))

    def ring_product(m):
        block = product("ring", m)
        for e in range(2):
            top, low = block[:half, e * LANES:(e + 1) * LANES], block[half:, e * LANES:(e + 1) * LANES]
            first = jnp.where(left, top, swap(low))
            second = jnp.where(left, swap(top), low)
            cx_own[m, e] = jnp.where(core == 0, first, second)
            cx_send[m, e] = jnp.where(core == 0, second, first)
        cx[m] = send(cx_send.at[m], cx_recv.at[m], cx_ssem.at[m], cx_rsem.at[m], sibling)

    def ring_pass(m):
        cx[m].wait_recv()
        if m:
            for e in range(2):
                zs_send[m, e] = (cx_own[m, e] + cx_recv[m, e]).astype(bf16)
                zs[m, e] = send(zs_send.at[m, e], zs_recv.at[z], zs_ssem.at[m, e],
                                zs_rsem.at[PAIRS - m, odd], ring(in_pair(m, e)))
        else:
            zs_send[0, 0] = (cx_own[0, 1 - odd] + cx_recv[0, 1 - odd]).astype(bf16)
            zs[0, 0] = send(zs_send.at[0, 0], zs_recv.at[z], zs_ssem.at[0, 0],
                            zs_rsem.at[0, odd], ring(in_pair(0, 1 - odd)))
            zs_recv[z] = (cx_own[0, odd] + cx_recv[0, odd]).astype(bf16)

    for m in LINE_ORDER[:1]:
        line_product(m)
    pl.semaphore_wait(barrier, RING - 1 + PLANE - 1 + 1)

    @pl.when(near)
    def _():
        for copy in t_out:
            copy.start()

    for m in LINE_ORDER[:1]:
        line_swap(m)
    line_product(LINE_ORDER[1])
    line_swap(LINE_ORDER[1])
    line_product(LINE_ORDER[2])
    line_swap(LINE_ORDER[2])
    line_pass(LINE_ORDER[0])
    line_product(LINE_ORDER[3])
    line_swap(LINE_ORDER[3])
    line_pass(LINE_ORDER[1])
    ring_product(ORDER[0])
    line_pass(LINE_ORDER[2])
    ring_product(ORDER[1])
    line_pass(LINE_ORDER[3])
    for i in range(2, PAIRS):
        ring_product(ORDER[i])
        pl.when(near)(functools.partial(t_pass, i - 2))

    @pl.when(near)
    def _():
        for i in range(2, PIECES):
            t_pass(i)

    for copy in lz.values():
        copy.wait_send()
    for m in ORDER:
        ring_pass(m)

    load_ts.wait()
    load_fs.wait()
    tcol[...] = jnp.broadcast_to(ts_ref[...][None, :], (LANES, n_basis)).T
    load_t.wait()

    lc, lp, ls, lm, lf = {}, {}, {}, {}, {}
    cs, ss, ms, fw = {}, {}, {}, {}
    mine_r = (x * 4 + y) * part
    own_r = pl.ds(pl.multiple_of(mine_r, part), part)
    small_r = (x * 4 + y) * small
    own_s = pl.ds(pl.multiple_of(small_r, small), small)
    own_s2 = pl.ds(pl.multiple_of(mid + small_r, small), small)

    def line_mm2():
        total = lx_own[0] + lx_recv[0]
        for m in reversed(LINE_ORDER[:-1]):
            lz[m].wait_recv()
            total = total + lz_recv[m].astype(f32)
        lc_send[...] = lax.dot_general(t2[0], total.astype(bf16), contract, preferred_element_type=f32).astype(bf16)
        for q in PLANE_FAR_FIRST:
            src = lc_send.at[pl.ds(pl.multiple_of(plane_index(q) * part, part), part)]
            lc[q] = send(src, lc_recv.at[q], lc_ssem.at[q], lc_rsem.at[q], plane(q))

    def line_trade():
        total = lc_send[own_r].astype(f32)
        for q in reversed(PLANE_FAR_FIRST):
            lc[q].wait_recv()
            total = total + lc_recv[q].astype(f32)
        lp_send[...] = total.astype(bf16)
        lp[0] = send(lp_send, lp_recv, lp_ssem.at[0], lp_rsem.at[0], ring(z ^ 7))
        return total

    def line_scale(total):
        own_f = fs_ref[pl.ds(pl.multiple_of(owner * 256 + core * LANES, LANES), LANES)][None, :]
        denom = tcol[own_r] + own_f + noise_var
        lp[0].wait_recv()
        scaled = ((total + lp_recv[...].astype(f32)) / denom).astype(bf16)
        ls_own[...] = scaled
        ls_all[own_r] = scaled
        for q in PLANE_FAR_FIRST:
            ls[q] = send(ls_own, ls_all.at[own_r], ls_ssem.at[q], ls_rsem.at[q], plane(q))

    def line_mm3():
        for q in reversed(PLANE_FAR_FIRST):
            ls[q].wait_recv()
        mixed = jnp.dot(t2[0], ls_all[...], preferred_element_type=f32).astype(bf16)
        lm_send[...] = mixed
        lm_all[0, core] = mixed
        for m in LINE_ORDER[:-1]:
            lm[m] = send(lm_send, lm_all.at[m, core], lm_ssem.at[m], lm_rsem.at[m], line(m))

    def line_forward(m):
        if m:
            lm[m].wait_recv()
        slot = lm_all.at[m, core]
        lf[m] = send(slot, slot, lf_ssem.at[m], lf_rsem.at[m], sibling)

    def line_mm4(m):
        lf[m].wait_recv()
        block = jnp.concatenate([lm_all[m, 0], lm_all[m, 1]], axis=1)
        return jnp.dot(block, featst[0, m], preferred_element_type=f32)

    def wait_ring(sem, src, dst):
        for m in range(1, PAIRS):
            for e in range(2):
                remote(src, dst, sem.at[m, e], sem.at[m, e], sibling).wait_recv()
        other = sem.at[0, 1 - odd]
        remote(src, dst, other, other, sibling).wait_recv()

    def ring_mm2():
        wait_ring(zs_rsem, zs_send.at[0, 0], zs_recv.at[0])
        total = None
        for g in range(2):
            base = (zh if g == 0 else 1 - zh) * 4
            packed = ((zs_recv[base].astype(f32) + zs_recv[base + 1].astype(f32))
                      + (zs_recv[base + 2].astype(f32) + zs_recv[base + 3].astype(f32)))
            swapped = swap(packed)
            low = jnp.concatenate([jnp.where(left, packed, 0), jnp.where(left, swapped, 0)], axis=0).astype(bf16)
            high = jnp.concatenate([jnp.where(left, 0, swapped), jnp.where(left, 0, packed)], axis=0).astype(bf16)
            add = (lax.dot_general(t2[g, :, :mid], low, contract, preferred_element_type=f32)
                   + lax.dot_general(t2[g, :, mid:], high, contract, preferred_element_type=f32))
            total = add if total is None else total + add
        c_send[...] = total.astype(bf16)
        for q in PLANE_FAR_FIRST:
            src = c_send.at[pl.ds(pl.multiple_of(plane_index(q) * small, small), small)]
            cs[q] = send(src, c_recv.at[q], c_ssem.at[q], c_rsem.at[q], plane(q))

    def ring_scale():
        total = c_send[own_s].astype(f32)
        own_f = fs_ref[pl.ds(pl.multiple_of(width + z * LANES, LANES), LANES)][None, :]
        other_f = swap(jnp.broadcast_to(own_f, (8, LANES)))[:1]
        both = jnp.where(left == (core == 0), own_f, other_f)
        denom = jnp.where(left, tcol[own_s], tcol[own_s2]) + both + noise_var
        for q in reversed(PLANE_FAR_FIRST):
            cs[q].wait_recv()
            total = total + c_recv[q].astype(f32)
        scaled = (total / denom).astype(bf16)
        s_own[...] = scaled
        s_all[own_s] = scaled
        for q in PLANE_FAR_FIRST:
            ss[q] = send(s_own, s_all.at[own_s], s_ssem.at[q], s_rsem.at[q], plane(q))

    def ring_mm3():
        for q in reversed(PLANE_FAR_FIRST):
            ss[q].wait_recv()
        for g in range(2):
            first = jnp.dot(t2[g, :, :mid], s_all[...], preferred_element_type=f32)
            second = jnp.dot(t2[g, :, mid:], s_all[...], preferred_element_type=f32)
            both = jnp.where(left, first, second)
            both = both + swap(both)
            m_send[g] = jnp.where(left, both[:half], both[half:]).astype(bf16)
        for m in ORDER[:-1]:
            for e in range(2):
                dest = in_pair(m, e)
                ms[m, e] = send(m_send.at[(dest >> 2) ^ zh], m_all.at[PAIRS - m, odd, core],
                                m_ssem.at[m, e], m_rsem.at[PAIRS - m, odd], ring(dest))
        ms[0, 0] = send(m_send.at[0], m_all.at[0, odd, core],
                        m_ssem.at[0, 0], m_rsem.at[0, odd], ring(in_pair(0, 1 - odd)))
        m_all[0, odd, core] = m_send[0]

    def ring_forward(m):
        for i in range(2):
            e = i ^ odd if m == 0 else i
            slot = m_all.at[m, e, core]
            if m or i:
                sem = m_rsem.at[m, e]
                remote(slot, slot, sem, sem, sibling).wait_recv()
            fw[m, i] = send(slot, slot, f_ssem.at[m, e], f_rsem.at[m, e], sibling)

    def ring_mm4(m):
        sides = []
        for e in range(2):
            slot = m_all.at[m, e, core]
            remote(slot, slot, f_ssem.at[m, e], f_rsem.at[m, e], sibling).wait_recv()
            first, second = m_all[m, e, 0].astype(f32), m_all[m, e, 1].astype(f32)
            sides.append(jnp.concatenate([jnp.where(left, first, swap(second)),
                                          jnp.where(left, swap(first), second)], axis=0).astype(bf16))
        return jnp.dot(jnp.concatenate(sides, axis=1), featst[1, m], preferred_element_type=f32)

    def turn(k):
        for m in range(PAIRS):
            featst[k, m] = feats[k, m].T

    def sent(*groups):
        for copies in groups:
            for copy in copies.values():
                copy.wait_send()

    line_mm2()

    @pl.when(jnp.logical_not(near))
    def _():
        for i in range(PIECES):
            t_out[i].wait_recv()
            t_sib[i].start()

    turn(0)
    sent(lx, cx)
    line_sum = line_trade()
    for i in range(PIECES):
        t_sib[i].wait_recv()
    ring_mm2()
    sent(lc)
    line_scale(line_sum)
    turn(1)
    sent(zs, lp)
    ring_scale()
    sent(cs)

    @pl.when(near)
    def _():
        for copy in t_out + t_on:
            copy.wait_send()

    for copy in t_sib:
        copy.wait_send()
    line_mm3()
    sent(ls)
    ring_mm3()
    sent(ss)
    last = [("line", m) for m in reversed(LINE_ORDER)] + [("ring", m) for m in (0, 1, 3, 2)]
    for i in range(len(last) + 1):
        if i < len(last):
            (line_forward if last[i][0] == "line" else ring_forward)(last[i][1])
        if i == 0:
            continue
        if i == PAIRS + 1:
            sent(lm)
        if i == len(last):
            sent(lf, ms)
        kind, m = last[i - 1]
        add = line_mm4(m) if kind == "line" else ring_mm4(m)
        if i == 1:
            acc[...] = add
        elif i < len(last):
            acc[...] += add
        else:
            out[...] = (acc[...] + add).astype(out.dtype)
    sent(fw)


def per_device(fields, basis, features, time_spectrum, feature_spectrum):
    rows, sites = fields.shape
    half = rows // 2
    n_basis = basis.shape[1]
    mid = n_basis // 2
    part = n_basis // PLANE
    small = mid // PLANE
    any_space = pl.BlockSpec(memory_space=pl.ANY)
    vmem = pltpu.VMEM
    dma = pltpu.SemaphoreType.DMA
    return pl.pallas_call(
        kernel,
        out_shape=pltpu.VMEM((rows, sites), bf16),
        in_specs=[any_space] * 5,
        out_specs=pl.BlockSpec(memory_space=pltpu.VMEM),
        scratch_shapes=[
            vmem(time_spectrum.shape, f32),
            vmem(feature_spectrum.shape, f32),
            vmem((2, PAIRS, sites, 256), bf16),
            vmem((2, PAIRS, 256, sites), bf16),
            vmem((rows, sites), bf16),
            vmem((2, rows, n_basis), bf16),
            vmem((n_basis, LANES), f32),
            vmem((rows, sites), f32),
            vmem((PAIRS, rows, LANES), f32),
            vmem((PAIRS, rows, LANES), f32),
            vmem((PAIRS, rows, LANES), f32),
            vmem((PAIRS, rows, LANES), bf16),
            vmem((PAIRS, rows, LANES), bf16),
            vmem((n_basis, LANES), bf16),
            vmem((PLANE, part, LANES), bf16),
            vmem((part, LANES), bf16),
            vmem((part, LANES), bf16),
            vmem((part, LANES), bf16),
            vmem((n_basis, LANES), bf16),
            vmem((rows, LANES), bf16),
            vmem((PAIRS, 2, rows, LANES), bf16),
            vmem((PAIRS, 2, half, LANES), f32),
            vmem((PAIRS, 2, half, LANES), f32),
            vmem((PAIRS, 2, half, LANES), f32),
            vmem((PAIRS, 2, half, LANES), bf16),
            vmem((RING, half, LANES), bf16),
            vmem((mid, LANES), bf16),
            vmem((PLANE, small, LANES), bf16),
            vmem((small, LANES), bf16),
            vmem((mid, LANES), bf16),
            vmem((2, half, LANES), bf16),
            vmem((PAIRS, 2, 2, half, LANES), bf16),
            dma((4,)), dma((2, PAIRS)),
            dma((2, PIECES)), dma((PIECES,)), dma((PIECES,)), dma((PIECES,)),
            dma((PAIRS,)), dma((PAIRS,)), dma((PAIRS,)), dma((PAIRS,)),
            dma((PLANE,)), dma((PLANE,)), dma((1,)), dma((1,)), dma((PLANE,)), dma((PLANE,)),
            dma((PAIRS,)), dma((PAIRS,)), dma((PAIRS,)), dma((PAIRS,)),
            dma((PAIRS,)), dma((PAIRS,)), dma((PAIRS, 2)), dma((PAIRS, 2)),
            dma((PLANE,)), dma((PLANE,)), dma((PLANE,)), dma((PLANE,)),
            dma((PAIRS, 2)), dma((PAIRS, 2)), dma((PAIRS, 2)), dma((PAIRS, 2)),
        ],
        compiler_params=pltpu.CompilerParams(
            collective_id=0, has_side_effects=True, vmem_limit_bytes=60 * 2**20),
        cost_estimate=pl.CostEstimate(flops=3_600_000_000, bytes_accessed=13_000_000, transcendentals=0),
        name="solve",
    )(fields, basis, features, time_spectrum, feature_spectrum)


def solution(mesh):
    in_specs = (P("hour", "site"), P("hour", None), P("site", None), P(), P())
    out_specs = P("hour", "site")
    return jax.shard_map(
        per_device, mesh=mesh, in_specs=in_specs, out_specs=out_specs, check_vma=False
    )
```
